256 devices in a mesh: pipe: 16 (over y_lo, z), dp: 8 (over x, core), tensor: 2 (over y_hi).
Axes of the slice: x: 4, y: 4 (y_hi: 2, y_lo: 2; y = y_hi * 2 + y_lo), z: 8, core: 2. Of those that a mesh axis runs over, the one named last changes fastest.
Arguments:
- layer_input: bfloat16 [16, 1024, 8192], P('pipe', 'dp'), may hold values from -6 to 6
- norm_gain: bfloat16 [16, 8192], P('pipe'), may hold values from 0.5 to 1.5
- kv_weight: bfloat16 [16, 2, 8192, 512], P('pipe', None, 'dp', 'tensor'), may hold values from -0.0625 to 0.0625
- queries: bfloat16 [16, 1024, 4096], P('pipe', 'dp', 'tensor'), may hold values from -170 to 170
- out_grad: bfloat16 [16, 1024, 4096], P('pipe', 'dp', 'tensor'), may hold values from -6 to 6
- top_grad: bfloat16 [1024, 8192], P('dp', 'tensor'), may hold values from -4 to 4
- segment_ids: int32 [1024], P('dp'), may hold values from 0 to 31, never falling along the last dimension, each value on 1 to 128 neighbouring positions
- scale_exp: int32 [16, 2, 64, 4], P('pipe', None, 'dp', 'tensor'), may hold values from 3 to 6
Outputs:
- input_grad: bfloat16 [16, 1024, 8192], P('pipe', 'dp', 'tensor')
- kv_weight_grad: bfloat16 [16, 2, 8192, 512], P('pipe', None, 'dp', 'tensor')
The draws below stay inside these ranges and needn't reach their ends.
Inputs may be any that keep to these rules, and one draw needn't show every extreme that they name: `segment_ids`: document numbers never fall; each document has 1 to 128 tokens.
All inputs are finite; a program needn't handle non-finite values.
Results may differ from the reference program's by a relative error of at most 0.019.
Values may be sent and summed in bfloat16 or wider, within the bound.
No kernel may reach another device: no remote copies, remote signals or barrier semaphores. Data moves between devices by JAX's collectives and lax.ppermute only.
A program may use at most 128 MiB of HBM per device.

```python
import math
import jax
import jax.numpy as jnp
import numpy as np
from jax import lax

D = 8192
HD = 128
Q_HEADS = 32
KV_HEADS = 4
BLOCK = 128
SPAN = 64
LAYERS = 16
TOK = 128
TOKENS = 1024


def draw_layer_input(key, part):
    key = jax.random.fold_in(key, 11)
    values = jnp.clip(jax.random.normal(key, (LAYERS, TOKENS, D), jnp.float32), -6.0, 6.0)
    return values.astype(jnp.bfloat16)


def draw_queries(key, part):
    key = jax.random.fold_in(key, 23)
    values = jnp.clip(jax.random.normal(key, (LAYERS, TOKENS, Q_HEADS * HD), jnp.float32), -6.0, 6.0)
    return values.astype(jnp.bfloat16)


def touch_ends(result, rng, least, top_value):
    shape = result.shape
    spot = [jax.random.randint(jax.random.fold_in(rng, axis), (), 0, shape[axis]) for axis in range(len(shape))]
    result = result.at[tuple(spot)].set(least)
    longest = shape.index(max(shape))
    spot[longest] = (spot[longest] + 1) % shape[longest]
    return result.at[tuple(spot)].set(top_value)


def level_of(rng, extent, cuts, low, high):
    factor_of, own = 1.0, jax.random.fold_in(rng, 6)
    for axis_at, shards_of in cuts:
        steps = jnp.exp(jax.random.uniform(jax.random.fold_in(own, axis_at), (shards_of,), jnp.float32, low / len(cuts), high / len(cuts)))
        factor_of = factor_of * jnp.repeat(steps, extent[axis_at] // shards_of).reshape([-1 if axis == axis_at else 1 for axis in range(len(extent))])
    return factor_of


def split_up(count, total, reach, skew):
    weights = [(1 << 20) // math.isqrt(grade ** skew) + 1 for grade in range(2, count + 1)]
    surplus, holding = total - reach - (count - 1), [1] * (count - 1)
    while surplus > 0:
        free = [i for i in range(count - 1) if holding[i] < reach]
        whole, remaining = sum([weights[i] for i in free]), surplus
        for i in free:
            addition = min(reach - holding[i], max(1, remaining * weights[i] // whole), surplus)
            holding[i] = holding[i] + addition
            surplus = surplus - addition
    return np.array([reach] + holding)


def uneven_parts(stream_key, amount, total, reach, lean):
    if amount == 2:
        one = jax.random.randint(stream_key, (), max(1, total - reach), min(reach, total - 1) + 1)
        return jnp.stack([one, total - one])
    tallies = jnp.asarray(split_up(amount, total, reach, lean), jnp.int32)
    couples = (amount - 1) // 2
    giver, taker = tallies[1:1 + 2 * couples:2], tallies[2:2 + 2 * couples:2]
    margin = jnp.minimum(giver - 1, reach - taker)
    shifted = jax.random.randint(jax.random.fold_in(stream_key, 1), (couples,), 0, 1 << 20) % (margin + 1)
    tallies = tallies.at[1:1 + 2 * couples:2].set(giver - shifted).at[2:2 + 2 * couples:2].set(taker + shifted)
    return tallies[jax.random.permutation(jax.random.fold_in(stream_key, 2), amount)]


def normal_values(stream_key, dims, width, bound, pieces=(), kind=jnp.bfloat16):
    values = jax.random.normal(stream_key, dims, jnp.float32) * width
    if len(pieces) > 0:
        values = level_of(stream_key, dims, pieces, -0.22, 0.18) * values
    return jnp.clip(values, min=-bound, max=bound).astype(kind)


def setup_inputs(seed: int = 0) -> dict:
    seeds = jax.random.split(jax.random.key(seed), 9)
    layer_input = draw_layer_input(jax.random.fold_in(seeds[8], 71), 0)
    norm_gain = jnp.clip(1.0 + 0.1 * jax.random.normal(seeds[1], (LAYERS, D), jnp.float32), 0.5, 1.5).astype(jnp.bfloat16)
    kv_weight = normal_values(seeds[2], (LAYERS, 2, D, KV_HEADS * HD), D ** -0.5, 0.0625, ((0, 16), (2, 8), (3, 2)))
    queries = draw_queries(jax.random.fold_in(seeds[8], 71), 0)
    out_grad = normal_values(seeds[4], (LAYERS, TOKENS, Q_HEADS * HD), 1.0, 6.0, ((0, 16), (1, 8), (2, 2)))
    top_grad = normal_values(seeds[5], (TOKENS, D), 0.25, 4.0, ((0, 8), (1, 2)))
    segment_ids = jnp.searchsorted(jnp.cumsum(uneven_parts(seeds[6], TOKENS // (SPAN // 2), TOKENS, TOK, 2)), jnp.arange(TOKENS), side="right").astype(jnp.int32)
    scale_exp = touch_ends(jax.random.randint(seeds[7], (LAYERS, 2, D // BLOCK, KV_HEADS), 3, 7), jax.random.fold_in(seeds[7], 1), 3, 6).astype(jnp.int32)
    return dict(layer_input=layer_input, norm_gain=norm_gain, kv_weight=kv_weight, queries=queries, out_grad=out_grad, top_grad=top_grad, segment_ids=segment_ids, scale_exp=scale_exp)


EPS = 1e-05

def attend(query, grad_out, key_rows, value_rows, seg_query, seg_key, offset):
    count_q = query.shape[0]
    count_k = key_rows.shape[0]
    kv_local = key_rows.shape[1] // HD
    group_size = query.shape[1] // key_rows.shape[1]
    score_scale = HD ** (-0.5)
    query_h = query.astype(jnp.float32).reshape(count_q, kv_local, group_size, HD)
    grad_h = grad_out.astype(jnp.float32).reshape(count_q, kv_local, group_size, HD)
    key_h = key_rows.astype(jnp.float32).reshape(count_k, kv_local, HD)
    value_h = value_rows.astype(jnp.float32).reshape(count_k, kv_local, HD)
    scores = jnp.einsum('qkgd,mkd->kgqm', query_h, key_h) * score_scale
    query_pos = offset + jnp.arange(count_q, dtype=jnp.int32)
    key_pos = jnp.arange(count_k, dtype=jnp.int32)
    allowed = (key_pos[None, :] <= query_pos[:, None]) & (seg_key[None, :] == seg_query[:, None])
    scores = jnp.where(allowed, scores, jnp.float32(-1e+30))
    row_max = lax.optimization_barrier(jnp.max(scores, -1, keepdims=True))
    probability = jnp.exp(scores - row_max)
    probability = probability / lax.optimization_barrier(jnp.sum(probability, -1, keepdims=True))
    dprob = jnp.einsum('qkgd,mkd->kgqm', grad_h, value_h)
    delta = lax.optimization_barrier(jnp.sum(probability * dprob, -1, keepdims=True))
    dscore = probability * (dprob - delta)
    prob_b = lax.optimization_barrier(probability.astype(jnp.bfloat16)).astype(jnp.float32)
    dscore_b = lax.optimization_barrier(dscore.astype(jnp.bfloat16)).astype(jnp.float32)
    value_grad = jnp.einsum('kgqm,qkgd->mkd', prob_b, grad_h)
    key_grad = jnp.einsum('kgqm,qkgd->mkd', dscore_b, query_h) * score_scale
    return (key_grad.reshape(count_k, kv_local * HD), value_grad.reshape(count_k, kv_local * HD))

def reference(layer_input, norm_gain, kv_weight, queries, out_grad, top_grad, segment_ids, scale_exp):
    windows = TOKENS // TOK

    def layer_step(running, layer_data):
        inputs, gain_row, weights, query_all, grad_all, exponents = layer_data
        x_float = inputs.astype(jnp.float32)
        inv_rms = lax.rsqrt(lax.optimization_barrier(jnp.mean(x_float * x_float, -1, keepdims=True)) + EPS)
        x_hat = x_float * inv_rms
        gain_f = gain_row.astype(jnp.float32)
        normed = (x_hat * gain_f).astype(jnp.bfloat16)
        key_rows = jnp.dot(normed, weights[0], preferred_element_type=jnp.float32).astype(jnp.bfloat16)
        value_rows = jnp.dot(normed, weights[1], preferred_element_type=jnp.float32).astype(jnp.bfloat16)

        def one_window(query_w, grad_w, key_w, value_w, seg_w):
            return attend(query_w, grad_w, key_w, value_w, seg_w, seg_w, 0)
        key_grad, value_grad = jax.vmap(one_window)(query_all.reshape(windows, TOK, -1), grad_all.reshape(windows, TOK, -1), key_rows.reshape(windows, TOK, -1), value_rows.reshape(windows, TOK, -1), segment_ids.reshape(windows, TOK))
        key_b = key_grad.reshape(TOKENS, -1).astype(jnp.bfloat16)
        value_b = value_grad.reshape(TOKENS, -1).astype(jnp.bfloat16)
        d_normed = jnp.dot(key_b, weights[0].T, preferred_element_type=jnp.float32)
        d_normed = d_normed + jnp.dot(value_b, weights[1].T, preferred_element_type=jnp.float32)
        gated_grad = gain_f * d_normed
        inner_mean = lax.optimization_barrier(jnp.mean(gated_grad * x_hat, -1, keepdims=True))
        branch = inv_rms * (gated_grad - x_hat * inner_mean)
        running = running + branch
        grad_rows = running.astype(jnp.bfloat16)
        normed_w = normed.reshape(windows, TOK, D).astype(jnp.float32)

        def summed_parts(grads_b):
            parts = jnp.einsum('rtd,rtc->rdc', normed_w, grads_b.reshape(windows, TOK, -1).astype(jnp.float32))
            parts = lax.optimization_barrier(parts.astype(jnp.bfloat16)).astype(jnp.float32)
            return lax.optimization_barrier(jnp.sum(parts, 0))
        both_grads = jnp.stack([summed_parts(key_b), summed_parts(value_b)])
        factor = jnp.exp2(-exponents.astype(jnp.float32))
        factor = jnp.repeat(jnp.repeat(factor, BLOCK, 1), HD, 2)
        weight_grad = (both_grads * factor).astype(jnp.bfloat16)
        return (running, (grad_rows, weight_grad))
    start_grad = top_grad.astype(jnp.float32)
    final_grad, outputs = lax.scan(layer_step, start_grad, (layer_input, norm_gain, kv_weight, queries, out_grad, scale_exp), reverse=True)
    return (outputs[0], outputs[1])
```

```python
import jax
import jax.numpy as jnp
from jax import lax
from jax.experimental import pallas as pl
from jax.experimental.pallas import tpu as pltpu
from jax.sharding import PartitionSpec as P

HD = 128
BLOCK = 128
EPS = 1e-05


def attend(query, grad_out, key_rows, value_rows, segments):
    count = query.shape[0]
    kv_local = key_rows.shape[1] // HD
    group_size = query.shape[1] // key_rows.shape[1]
    score_scale = HD ** (-0.5)
    query_h = query.reshape(count, kv_local, group_size, HD)
    grad_h = grad_out.reshape(count, kv_local, group_size, HD)
    key_h = key_rows.reshape(count, kv_local, HD)
    value_h = value_rows.reshape(count, kv_local, HD)
    scores = (
        jnp.einsum("qkgd,mkd->kgqm", query_h, key_h, preferred_element_type=jnp.float32)
        * score_scale
    )
    pos = jnp.arange(count, dtype=jnp.int32)
    allowed = (pos[None, :] <= pos[:, None]) & (segments[None, :] == segments[:, None])
    scores = jnp.where(allowed, scores, jnp.float32(-1e30))
    row_max = jnp.max(scores, -1, keepdims=True)
    probability = jnp.exp(scores - row_max)
    probability = probability / jnp.sum(probability, -1, keepdims=True)
    dprob = jnp.einsum("qkgd,mkd->kgqm", grad_h, value_h, preferred_element_type=jnp.float32)
    delta = jnp.sum(probability * dprob, -1, keepdims=True)
    dscore_b = (probability * (dprob - delta)).astype(jnp.bfloat16)
    prob_b = probability.astype(jnp.bfloat16)
    value_grad = jnp.einsum("kgqm,qkgd->mkd", prob_b, grad_h, preferred_element_type=jnp.float32)
    key_grad = (
        jnp.einsum("kgqm,qkgd->mkd", dscore_b, query_h, preferred_element_type=jnp.float32)
        * score_scale
    )
    return (
        key_grad.reshape(count, kv_local * HD).astype(jnp.bfloat16),
        value_grad.reshape(count, kv_local * HD).astype(jnp.bfloat16),
    )


def suffix_kernel(parts_ref, top_ref, out_ref):
    layers = parts_ref.shape[0]
    running = top_ref[...].astype(jnp.float32)
    for layer in reversed(range(layers)):
        running = running + parts_ref[layer].astype(jnp.float32)
        out_ref[layer] = running.astype(jnp.bfloat16)


def suffix_sum(parts, top):
    layers, rows, width = parts.shape
    tile = min(width, 1024)
    return pl.pallas_call(
        suffix_kernel,
        grid=(width // tile,),
        in_specs=[
            pl.BlockSpec((layers, rows, tile), lambda i: (0, 0, i)),
            pl.BlockSpec((rows, tile), lambda i: (0, i)),
        ],
        out_specs=pl.BlockSpec((layers, rows, tile), lambda i: (0, 0, i)),
        out_shape=jax.ShapeDtypeStruct(parts.shape, jnp.bfloat16),
        cost_estimate=pl.CostEstimate(
            flops=parts.size, bytes_accessed=4 * parts.size, transcendentals=0
        ),
    )(parts, top)


def on_device(
    layer_input, norm_gain, kv_weight, queries, out_grad, top_grad, segment_ids, scale_exp
):
    inputs = layer_input[0]
    weights = lax.all_gather(kv_weight[0], "dp", axis=1, tiled=True)
    token_count, feature_count = inputs.shape
    kv_width = weights.shape[2]
    half_width = feature_count // lax.axis_size("tensor")
    tensor_pos = lax.axis_index("tensor")
    pipe_count = lax.axis_size("pipe")
    pipe_pos = lax.axis_index("pipe")
    x_float = inputs.astype(jnp.float32)
    inv_rms = lax.rsqrt(jnp.mean(x_float * x_float, -1, keepdims=True) + EPS)
    x_hat = x_float * inv_rms
    gain_f = norm_gain[0].astype(jnp.float32)
    normed = (x_hat * gain_f).astype(jnp.bfloat16)
    key_f = jnp.dot(normed, weights[0], preferred_element_type=jnp.float32)
    value_f = jnp.dot(normed, weights[1], preferred_element_type=jnp.float32)
    key_b, value_b = attend(
        queries[0],
        out_grad[0],
        key_f.astype(jnp.bfloat16),
        value_f.astype(jnp.bfloat16),
        segment_ids,
    )
    inner = (
        jnp.sum(
            key_b.astype(jnp.float32) * key_f + value_b.astype(jnp.float32) * value_f,
            -1,
            keepdims=True,
        )
        / feature_count
    )

    def partial_branch(start):
        rows_k = lax.dynamic_slice_in_dim(weights[0], start, half_width, 0)
        rows_v = lax.dynamic_slice_in_dim(weights[1], start, half_width, 0)
        d_normed = jnp.einsum("tc,dc->td", key_b, rows_k, preferred_element_type=jnp.float32)
        d_normed = d_normed + jnp.einsum(
            "tc,dc->td", value_b, rows_v, preferred_element_type=jnp.float32
        )
        x_rows = lax.dynamic_slice_in_dim(inputs, start, half_width, 1).astype(jnp.float32)
        gains = lax.dynamic_slice_in_dim(gain_f, start, half_width, 0)
        return inv_rms * (gains * d_normed - (x_rows * inv_rms) * inner)

    theirs = partial_branch((1 - tensor_pos) * half_width).astype(jnp.bfloat16)
    arrived = lax.ppermute(theirs, "tensor", [(0, 1), (1, 0)])
    mine = partial_branch(tensor_pos * half_width)
    branch = (mine + arrived.astype(jnp.float32)).astype(jnp.bfloat16)
    parts = lax.all_to_all(branch, "pipe", 0, 0, tiled=True)
    rows = token_count // pipe_count
    top_rows = lax.dynamic_slice_in_dim(top_grad, pipe_pos * rows, rows, 0)
    sums = suffix_sum(parts.reshape(pipe_count, rows, half_width), top_rows)
    input_grad = lax.all_to_all(sums.reshape(token_count, half_width), "pipe", 0, 0, tiled=True)

    grads_b = jnp.concatenate([key_b, value_b], 1)
    summed = lax.psum_scatter(
        jnp.einsum("tr,tc->rc", normed, grads_b, preferred_element_type=jnp.float32).astype(
            jnp.bfloat16
        ),
        "dp",
        scatter_dimension=0,
        tiled=True,
    ).astype(jnp.float32)
    factor = jnp.exp2(-scale_exp[0].astype(jnp.float32))
    factor = jnp.repeat(jnp.repeat(factor, BLOCK, 1), HD, 2)
    both_grads = jnp.stack([summed[:, :kv_width], summed[:, kv_width:]])
    weight_grad = (both_grads * factor).astype(jnp.bfloat16)[None]
    return (input_grad[None], weight_grad)


def solution(mesh):
    placed = (
        P("pipe", "dp", None),
        P("pipe", None),
        P("pipe", None, "dp", "tensor"),
        P("pipe", "dp", "tensor"),
        P("pipe", "dp", "tensor"),
        P("dp", "tensor"),
        P("dp"),
        P("pipe", None, "dp", "tensor"),
    )
    return jax.shard_map(
        on_device,
        mesh=mesh,
        in_specs=placed,
        out_specs=(P("pipe", "dp", "tensor"), P("pipe", None, "dp", "tensor")),
        check_vma=False,
    )
```

```python
import jax
import jax.numpy as jnp
from jax import lax
from jax.experimental import pallas as pl
from jax.experimental.pallas import tpu as pltpu
from jax.sharding import PartitionSpec as P

HD = 128
BLOCK = 128
EPS = 1e-05
MIB = 1024 * 1024
TILE = 1024
HALF_TILES = 4
THEIRS, MINE, STAGE = 16, 17, 18

NT = (((1,), (1,)), ((), ()))
NN = (((1,), (0,)), ((), ()))
TN = (((0,), (0,)), ((), ()))


def dot(a, b, dims):
    return lax.dot_general(a, b, dims, preferred_element_type=jnp.float32)


def cost(flops, nbytes, transcendentals=0):
    return pl.CostEstimate(
        flops=int(flops), bytes_accessed=int(nbytes), transcendentals=int(transcendentals)
    )


def stacked(ref, group, count):
    base = group * count
    return jnp.concatenate([ref[:, (base + h) * HD : (base + h + 1) * HD] for h in range(count)], 0)


def add_rows(shards_ref, normed_ref, pieces, whole_ref, sems, first, total):
    depth = pieces[0].shape[0]
    copies = []
    for i, piece in enumerate(pieces):
        rows = pl.ds(pl.multiple_of(shards_ref[first + i] * depth, depth), depth)
        copy = pltpu.make_async_copy(piece, whole_ref.at[rows, :], sems.at[i])
        copy.start()
        copies.append(copy)
    for i, piece in enumerate(pieces):
        columns = pl.ds(pl.multiple_of(shards_ref[first + i] * depth, depth), depth)
        part = dot(normed_ref[:, columns], piece[...], NN)
        total = part if total is None else total + part
    return total, copies


def in_vmem(count):
    return [pl.BlockSpec(memory_space=pltpu.VMEM)] * count


IN_SMEM = pl.BlockSpec(memory_space=pltpu.SMEM)
ANYWHERE = pl.BlockSpec(memory_space=pl.ANY)


def places_kernel(out_ref):
    me = lax.axis_index("dp")
    tensor_pos = lax.axis_index("tensor")
    before, after, across = lax.rem(me + 6, 8), lax.rem(me + 2, 8), lax.rem(me + 4, 8)
    order = (me, before, me, after, after, across, before, across)
    for i, shard in enumerate(order):
        out_ref[2 * i] = shard
        out_ref[2 * i + 1] = shard + 1 - 2 * lax.rem(shard, 2)
    out_ref[THEIRS] = (1 - tensor_pos) * HALF_TILES
    out_ref[MINE] = tensor_pos * HALF_TILES
    out_ref[STAGE] = lax.axis_index("pipe")


def all_places():
    return pl.pallas_call(
        places_kernel,
        out_specs=IN_SMEM,
        out_shape=jax.ShapeDtypeStruct((32,), jnp.int32),
        compiler_params=pltpu.CompilerParams(vmem_limit_bytes=MIB),
        cost_estimate=cost(0, 0),
    )()


def normed_kernel(x_ref, gain_ref, normed_ref, rms_ref):
    x = x_ref[...].astype(jnp.float32)
    rms = lax.rsqrt(jnp.mean(x * x, -1, keepdims=True) + EPS)
    rms_ref[...] = rms
    normed_ref[...] = ((x * rms) * gain_ref[...].astype(jnp.float32)).astype(jnp.bfloat16)


def norm(x, gain):
    tokens, features = x.shape
    rows = min(tokens, 32)
    return pl.pallas_call(
        normed_kernel,
        grid=(tokens // rows,),
        in_specs=[
            pl.BlockSpec((rows, features), lambda i: (i, 0)),
            pl.BlockSpec((1, features), lambda i: (0, 0)),
        ],
        out_specs=[
            pl.BlockSpec((rows, features), lambda i: (i, 0)),
            pl.BlockSpec((rows, 1), lambda i: (i, 0)),
        ],
        out_shape=(
            jax.ShapeDtypeStruct(x.shape, jnp.bfloat16),
            jax.ShapeDtypeStruct((tokens, 1), jnp.float32),
        ),
        compiler_params=pltpu.CompilerParams(vmem_limit_bytes=12 * MIB),
        cost_estimate=cost(4 * x.size, 4 * x.size),
    )(x, gain)


def early_kernel(shards_ref, normed_ref, both_ref, *refs, count):
    key_pieces, value_pieces = list(refs[: count - 1]), list(refs[count - 1 : 2 * count - 2])
    key_pieces.insert(1, both_ref.at[0])
    value_pieces.insert(1, both_ref.at[1])
    key_ref, value_ref, key_w_ref, value_w_ref, key_sems, value_sems = refs[2 * count - 2 :]
    key_f, copies = add_rows(shards_ref, normed_ref, key_pieces, key_w_ref, key_sems, 0, None)
    value_f, more = add_rows(
        shards_ref, normed_ref, value_pieces, value_w_ref, value_sems, count, None
    )
    key_ref[...] = key_f
    value_ref[...] = value_f
    for copy in copies + more:
        copy.wait()


def early_rows(shards, normed, both, key_pieces, value_pieces):
    tokens, features = normed.shape
    depth, width = key_pieces[0].shape
    count = len(key_pieces) + 1
    rows = jax.ShapeDtypeStruct((tokens, width), jnp.float32)
    whole = jax.ShapeDtypeStruct((features, width), jnp.bfloat16)
    return pl.pallas_call(
        lambda *refs: early_kernel(*refs, count=count),
        in_specs=[IN_SMEM] + in_vmem(2 * count),
        out_specs=in_vmem(2) + [ANYWHERE] * 2,
        out_shape=(rows, rows, whole, whole),
        scratch_shapes=[pltpu.SemaphoreType.DMA((count,))] * 2,
        compiler_params=pltpu.CompilerParams(vmem_limit_bytes=16 * MIB),
        cost_estimate=cost(4 * tokens * depth * width * count, 8 * depth * width * count),
    )(shards, normed, both, *key_pieces, *value_pieces)


def attention_kernel(shards_ref, normed_ref, *refs, count, first, features):
    key_pieces, value_pieces = refs[:count], refs[count : 2 * count]
    key_part_ref, value_part_ref, _, _, query_ref, grad_ref, seg_ref = refs[
        2 * count : 2 * count + 7
    ]
    key_w_ref, value_w_ref, key_grad_ref, value_grad_ref, inner_ref, key_sems, value_sems = refs[
        2 * count + 7 :
    ]
    key_f, copies = add_rows(
        shards_ref, normed_ref, key_pieces, key_w_ref, key_sems, first, key_part_ref[...]
    )
    value_f, more = add_rows(
        shards_ref, normed_ref, value_pieces, value_w_ref, value_sems, first + count, value_part_ref[...]
    )
    tokens = query_ref.shape[0]
    width = key_f.shape[1]
    group_size = query_ref.shape[1] // width
    key_pos = lax.broadcasted_iota(jnp.int32, (tokens, tokens), 0)
    query_pos = lax.broadcasted_iota(jnp.int32, (tokens, tokens), 1)
    by_query = jnp.broadcast_to(seg_ref[...].astype(jnp.float32), (tokens, tokens))
    allowed = (key_pos <= query_pos) & (by_query.T == by_query)
    allowed = jnp.concatenate([jnp.where(allowed, 1.0, 0.0)] * group_size, 1) > 0.5
    total = jnp.zeros(inner_ref.shape, jnp.float32)
    for j in range(width // HD):
        at = slice(j * HD, (j + 1) * HD)
        key_j, value_j = key_f[:, at], value_f[:, at]
        query_j = stacked(query_ref, j, group_size)
        grad_j = stacked(grad_ref, j, group_size)
        scores = dot(key_j.astype(jnp.bfloat16), query_j, NT) * (HD ** (-0.5))
        scores = jnp.where(allowed, scores, jnp.float32(-1e30))
        weight = jnp.exp(scores - jnp.max(scores, 0, keepdims=True))
        probability = weight / jnp.sum(weight, 0, keepdims=True)
        value_grad = dot(probability.astype(jnp.bfloat16), grad_j, NN).astype(jnp.bfloat16)
        dprob = dot(value_j.astype(jnp.bfloat16), grad_j, NT)
        delta = jnp.sum(probability * dprob, 0, keepdims=True)
        dscore_b = (probability * (dprob - delta)).astype(jnp.bfloat16)
        key_grad = (dot(dscore_b, query_j, NN) * (HD ** (-0.5))).astype(jnp.bfloat16)
        key_grad_ref[:, at] = key_grad
        value_grad_ref[:, at] = value_grad
        total = total + jnp.sum(
            key_grad.astype(jnp.float32) * key_j + value_grad.astype(jnp.float32) * value_j,
            1,
            keepdims=True,
        )
    inner_ref[...] = total / features
    for copy in copies + more:
        copy.wait()


def attention_grads(shards, first, normed, key_pieces, value_pieces, early, query, grad_out, segments):
    tokens, features = normed.shape
    depth, width = key_pieces[0].shape
    count = len(key_pieces)
    whole = jax.ShapeDtypeStruct((features, width), jnp.bfloat16)
    grads = jax.ShapeDtypeStruct((tokens, width), jnp.bfloat16)
    at = 2 * count + 4
    return pl.pallas_call(
        lambda *refs: attention_kernel(*refs, count=count, first=first, features=features),
        in_specs=[IN_SMEM] + in_vmem(2 * count + 3) + [ANYWHERE] * 2 + in_vmem(3),
        out_specs=[ANYWHERE] * 2 + in_vmem(3),
        out_shape=(whole, whole, grads, grads, jax.ShapeDtypeStruct((tokens, 1), jnp.float32)),
        input_output_aliases={at: 0, at + 1: 1},
        scratch_shapes=[pltpu.SemaphoreType.DMA((count,))] * 2,
        compiler_params=pltpu.CompilerParams(vmem_limit_bytes=20 * MIB),
        cost_estimate=cost(
            4 * tokens * depth * width * count + 8 * tokens * query.size,
            8 * depth * width * count + 4 * query.size,
            tokens * query.size // HD,
        ),
    )(shards, normed, *key_pieces, *value_pieces, *early, query, grad_out, segments)


def ordered_kernel(*refs):
    del refs


def ordered(arrays, after):
    count = len(arrays)
    return pl.pallas_call(
        ordered_kernel,
        in_specs=[ANYWHERE] * (count + 1),
        out_specs=[ANYWHERE] * count,
        out_shape=[jax.ShapeDtypeStruct(a.shape, a.dtype) for a in arrays],
        input_output_aliases={i: i for i in range(count)},
        compiler_params=pltpu.CompilerParams(vmem_limit_bytes=MIB),
        cost_estimate=cost(0, 0),
    )(*arrays, after)


def branch_kernel(
    at_ref, key_grad_ref, value_grad_ref, key_w_ref, value_w_ref, x_ref, gain_ref, rms_ref, inner_ref, out_ref
):
    d_normed = dot(key_grad_ref[...], key_w_ref[...], NT)
    d_normed = d_normed + dot(value_grad_ref[...], value_w_ref[...], NT)
    rms = rms_ref[...]
    x_hat = x_ref[...].astype(jnp.float32) * rms
    gated = gain_ref[...].astype(jnp.float32) * d_normed
    out_ref[...] = (rms * (gated - x_hat * inner_ref[...])).astype(out_ref.dtype)


def partial_branch(places, half, kind, key_grad, value_grad, key_w, value_w, x, gain, inv_rms, inner):
    tokens, columns = key_grad.shape
    tile, width = TILE, TILE * HALF_TILES
    whole = lambda i, at: (0, 0)
    rows = lambda i, at: (at[half] + i, 0)
    lanes = lambda i, at: (0, at[half] + i)
    return pl.pallas_call(
        branch_kernel,
        grid_spec=pltpu.PrefetchScalarGridSpec(
            num_scalar_prefetch=1,
            grid=(width // tile,),
            in_specs=[
                pl.BlockSpec((tokens, columns), whole),
                pl.BlockSpec((tokens, columns), whole),
                pl.BlockSpec((tile, columns), rows),
                pl.BlockSpec((tile, columns), rows),
                pl.BlockSpec((tokens, tile), lanes),
                pl.BlockSpec((1, tile), lanes),
                pl.BlockSpec((tokens, 1), whole),
                pl.BlockSpec((tokens, 1), whole),
            ],
            out_specs=pl.BlockSpec((tokens, tile), lambda i, at: (0, i)),
        ),
        out_shape=jax.ShapeDtypeStruct((tokens, width), kind),
        compiler_params=pltpu.CompilerParams(vmem_limit_bytes=8 * MIB),
        cost_estimate=cost(
            4 * tokens * width * columns, 4 * width * columns + 2 * width * tokens
        ),
    )(places, key_grad, value_grad, key_w, value_w, x, gain, inv_rms, inner)


def weight_part_kernel(normed_ref, key_grad_ref, value_grad_ref, after_ref, out_ref, token_ref):
    columns = key_grad_ref.shape[1]
    normed = normed_ref[...]
    out_ref[:, :columns] = dot(normed, key_grad_ref[...], TN).astype(out_ref.dtype)
    out_ref[:, columns:] = dot(normed, value_grad_ref[...], TN).astype(out_ref.dtype)
    token_ref[...] = jnp.zeros_like(token_ref)


def weight_part(normed, key_grad, value_grad, after):
    tokens, features = normed.shape
    columns = key_grad.shape[1]
    return pl.pallas_call(
        weight_part_kernel,
        grid=(features // TILE,),
        in_specs=[
            pl.BlockSpec((tokens, TILE), lambda i: (0, i)),
            pl.BlockSpec((tokens, columns), lambda i: (0, 0)),
            pl.BlockSpec((tokens, columns), lambda i: (0, 0)),
            ANYWHERE,
        ],
        out_specs=[
            pl.BlockSpec((TILE, 2 * columns), lambda i: (i, 0)),
            pl.BlockSpec((8, 128), lambda i: (0, 0)),
        ],
        out_shape=(
            jax.ShapeDtypeStruct((features, 2 * columns), jnp.bfloat16),
            jax.ShapeDtypeStruct((8, 128), jnp.float32),
        ),
        compiler_params=pltpu.CompilerParams(vmem_limit_bytes=8 * MIB),
        cost_estimate=cost(4 * tokens * features * columns, 4 * features * columns),
    )(normed, key_grad, value_grad, after)


def add_kernel(mine_ref, arrived_ref, token_ref, out_ref):
    out_ref[...] = (mine_ref[...] + arrived_ref[...].astype(jnp.float32)).astype(out_ref.dtype)


def add_halves(mine, arrived, token):
    tokens, width = mine.shape
    spec = pl.BlockSpec((tokens, TILE), lambda i: (0, i))
    return pl.pallas_call(
        add_kernel,
        grid=(width // TILE,),
        in_specs=[spec, spec, ANYWHERE],
        out_specs=spec,
        out_shape=jax.ShapeDtypeStruct(mine.shape, jnp.bfloat16),
        compiler_params=pltpu.CompilerParams(vmem_limit_bytes=8 * MIB),
        cost_estimate=cost(mine.size, 8 * mine.size),
    )(mine, arrived, token)


def copy_kernel(at_ref, in_ref, out_ref):
    out_ref[...] = in_ref[...]


def take_rows(places, array, rows):
    width = array.shape[1]
    return pl.pallas_call(
        copy_kernel,
        grid_spec=pltpu.PrefetchScalarGridSpec(
            num_scalar_prefetch=1,
            grid=(1,),
            in_specs=[pl.BlockSpec((rows, width), lambda i, at: (at[STAGE], 0))],
            out_specs=pl.BlockSpec((rows, width), lambda i, at: (0, 0)),
        ),
        out_shape=jax.ShapeDtypeStruct((rows, width), array.dtype),
        compiler_params=pltpu.CompilerParams(vmem_limit_bytes=MIB),
        cost_estimate=cost(0, 0),
    )(places, array)


def suffix_kernel(parts_ref, top_ref, out_ref):
    running = top_ref[...].astype(jnp.float32)
    for layer in reversed(range(parts_ref.shape[0])):
        running = running + parts_ref[layer].astype(jnp.float32)
        out_ref[layer] = running.astype(jnp.bfloat16)


def suffix_sum(parts, top):
    layers, rows, width = parts.shape
    tile = min(width, 1024)
    return pl.pallas_call(
        suffix_kernel,
        grid=(width // tile,),
        in_specs=[
            pl.BlockSpec((layers, rows, tile), lambda i: (0, 0, i)),
            pl.BlockSpec((rows, tile), lambda i: (0, i)),
        ],
        out_specs=pl.BlockSpec((layers, rows, tile), lambda i: (0, 0, i)),
        out_shape=jax.ShapeDtypeStruct(parts.shape, jnp.bfloat16),
        compiler_params=pltpu.CompilerParams(vmem_limit_bytes=8 * MIB),
        cost_estimate=cost(1e15, 1e12),
    )(parts, top)


def scale_kernel(factor_ref, summed_ref, out_ref):
    p = pl.program_id(0)
    for i in range(out_ref.shape[1] // BLOCK):
        for c in range(out_ref.shape[2] // HD):
            block = summed_ref[i * BLOCK : (i + 1) * BLOCK, c * HD : (c + 1) * HD]
            scaled = block.astype(jnp.float32) * factor_ref[p, i, c]
            out_ref[0, i * BLOCK : (i + 1) * BLOCK, c * HD : (c + 1) * HD] = scaled.astype(jnp.bfloat16)


def scaled_grad(summed, factor):
    rows = summed.shape[0]
    columns = summed.shape[1] // 2
    return pl.pallas_call(
        scale_kernel,
        grid=(2,),
        in_specs=[
            pl.BlockSpec(memory_space=pltpu.SMEM),
            pl.BlockSpec((rows, columns), lambda p: (0, p)),
        ],
        out_specs=pl.BlockSpec((1, rows, columns), lambda p: (p, 0, 0)),
        out_shape=jax.ShapeDtypeStruct((2, rows, columns), jnp.bfloat16),
        compiler_params=pltpu.CompilerParams(vmem_limit_bytes=8 * MIB),
        cost_estimate=cost(summed.size, 4 * summed.size),
    )(factor, summed)


def ring_pairs(count):
    right = [(i, (i + 2) % count) for i in range(count)]
    left = [(i, (i - 2) % count) for i in range(count)]
    other = [(i, i ^ 1) for i in range(count)]
    return right, left, other


def on_device(
    layer_input, norm_gain, kv_weight, queries, out_grad, top_grad, segment_ids, scale_exp
):
    inputs = layer_input[0]
    token_count, feature_count = inputs.shape
    pipe_count = lax.axis_size("pipe")
    right, left, other = ring_pairs(lax.axis_size("dp"))
    send = lambda piece, pairs: lax.ppermute(piece, "dp", pairs)
    key_own, value_own = kv_weight[0, 0], kv_weight[0, 1]
    key_l = send(key_own, right)
    value_r = send(value_own, left)
    both = send(kv_weight[0], other)
    key_r = send(key_own, left)
    value_l = send(value_own, right)
    key_2 = send(key_l, right)
    value_2 = send(value_r, left)

    places = all_places()
    normed, inv_rms = norm(inputs, norm_gain)
    early = early_rows(
        places,
        normed,
        both,
        [key_own, key_l, send(key_l, other)],
        [value_own, value_r, send(value_r, other)],
    )
    key_r, value_l = ordered((key_r, value_l), early[0])
    key_w, value_w, key_grad, value_grad, inner = attention_grads(
        places,
        8,
        normed,
        [key_r, send(key_r, other), key_2, send(key_2, other)],
        [value_l, send(value_l, other), value_2, send(value_2, other)],
        early,
        queries[0],
        out_grad[0],
        segment_ids[None, :],
    )

    def share(half, kind):
        return partial_branch(
            places, half, kind, key_grad, value_grad, key_w, value_w, inputs, norm_gain, inv_rms, inner
        )

    arrived = lax.ppermute(share(THEIRS, jnp.bfloat16), "tensor", [(0, 1), (1, 0)])
    mine = share(MINE, jnp.float32)
    part, token = weight_part(normed, key_grad, value_grad, mine)
    branch = add_halves(mine, arrived, token)
    parts = lax.all_to_all(branch, "pipe", 0, 0, tiled=True)
    rows = token_count // pipe_count
    sums = suffix_sum(
        parts.reshape(pipe_count, rows, branch.shape[1]), take_rows(places, top_grad, rows)
    )
    input_grad = lax.all_to_all(
        sums.reshape(token_count, branch.shape[1]), "pipe", 0, 0, tiled=True
    )

    summed = lax.psum_scatter(part, "dp", scatter_dimension=0, tiled=True)
    weight_grad = scaled_grad(summed, jnp.exp2(-scale_exp[0].astype(jnp.float32)))
    return (input_grad[None], weight_grad[None])


def solution(mesh):
    placed = (
        P("pipe", "dp", None),
        P("pipe", None),
        P("pipe", None, "dp", "tensor"),
        P("pipe", "dp", "tensor"),
        P("pipe", "dp", "tensor"),
        P("dp", "tensor"),
        P("dp"),
        P("pipe", None, "dp", "tensor"),
    )
    return jax.shard_map(
        on_device,
        mesh=mesh,
        in_specs=placed,
        out_specs=(P("pipe", "dp", "tensor"), P("pipe", None, "dp", "tensor")),
        check_vma=False,
    )
```

```python
import jax
import jax.numpy as jnp
from jax import lax
from jax.experimental import pallas as pl
from jax.experimental.pallas import tpu as pltpu
from jax.sharding import PartitionSpec as P

HD = 128
BLOCK = 128
EPS = 1e-05
MIB = 1024 * 1024
TILE = 1024
HALF_TILES = 4
THEIRS, MINE, STAGE, CORE, CHIP = 16, 17, 18, 19, 20

NT = (((1,), (1,)), ((), ()))
NN = (((1,), (0,)), ((), ()))
TN = (((0,), (0,)), ((), ()))


def dot(a, b, dims):
    return lax.dot_general(a, b, dims, preferred_element_type=jnp.float32)


def cost(flops, nbytes, transcendentals=0):
    return pl.CostEstimate(
        flops=int(flops), bytes_accessed=int(nbytes), transcendentals=int(transcendentals)
    )


def stacked(ref, group, count):
    base = group * count
    return jnp.concatenate([ref[:, (base + h) * HD : (base + h + 1) * HD] for h in range(count)], 0)


def add_rows(shards_ref, normed_ref, pieces, whole_ref, sems, first, total):
    depth = pieces[0].shape[0]
    copies = []
    for i, piece in enumerate(pieces):
        rows = pl.ds(pl.multiple_of(shards_ref[first + i] * depth, depth), depth)
        copy = pltpu.make_async_copy(piece, whole_ref.at[rows, :], sems.at[i])
        copy.start()
        copies.append(copy)
    for i, piece in enumerate(pieces):
        columns = pl.ds(pl.multiple_of(shards_ref[first + i] * depth, depth), depth)
        part = dot(normed_ref[:, columns], piece[...], NN)
        total = part if total is None else total + part
    return total, copies


def in_vmem(count):
    return [pl.BlockSpec(memory_space=pltpu.VMEM)] * count


IN_SMEM = pl.BlockSpec(memory_space=pltpu.SMEM)
ANYWHERE = pl.BlockSpec(memory_space=pl.ANY)


def places_kernel(out_ref):
    me = lax.axis_index("dp")
    tensor_pos = lax.axis_index("tensor")
    before, after, across = lax.rem(me + 6, 8), lax.rem(me + 2, 8), lax.rem(me + 4, 8)
    sibling = lambda shard: shard + 1 - 2 * lax.rem(shard, 2)
    order = (me, sibling(me), before, sibling(before), after)
    order += (me, sibling(me), after, sibling(after), before)
    order += (sibling(after), across, sibling(across))
    order += (sibling(before), across, sibling(across))
    for i, shard in enumerate(order):
        out_ref[i] = shard
    out_ref[CORE] = lax.rem(me, 2)
    out_ref[CHIP] = me // 2
    out_ref[THEIRS] = (1 - tensor_pos) * HALF_TILES
    out_ref[MINE] = tensor_pos * HALF_TILES
    out_ref[STAGE] = lax.axis_index("pipe")


def all_places():
    return pl.pallas_call(
        places_kernel,
        out_specs=IN_SMEM,
        out_shape=jax.ShapeDtypeStruct((32,), jnp.int32),
        compiler_params=pltpu.CompilerParams(vmem_limit_bytes=MIB),
        cost_estimate=cost(0, 0),
    )()


def normed_kernel(at_ref, x_ref, gain_ref, normed_ref, rms_ref, other_ref):
    x = x_ref[...].astype(jnp.float32)
    rms = lax.rsqrt(jnp.mean(x * x, -1, keepdims=True) + EPS)
    rms_ref[...] = rms
    normed_ref[...] = ((x * rms) * gain_ref[...].astype(jnp.float32)).astype(jnp.bfloat16)
    for k in range(other_ref.shape[1] // TILE):
        shard = 2 * k + 1 - at_ref[CORE]
        columns = pl.ds(pl.multiple_of(shard * TILE, TILE), TILE)
        other_ref[:, k * TILE : (k + 1) * TILE] = normed_ref[:, columns]


def norm(places, x, gain):
    tokens, features = x.shape
    rows = min(tokens, 32)
    by_rows = lambda i, at: (i, 0)
    return pl.pallas_call(
        normed_kernel,
        grid_spec=pltpu.PrefetchScalarGridSpec(
            num_scalar_prefetch=1,
            grid=(tokens // rows,),
            in_specs=[
                pl.BlockSpec((rows, features), by_rows),
                pl.BlockSpec((1, features), lambda i, at: (0, 0)),
            ],
            out_specs=[
                pl.BlockSpec((rows, features), by_rows),
                pl.BlockSpec((rows, 1), by_rows),
                pl.BlockSpec((rows, features // 2), by_rows),
            ],
        ),
        out_shape=(
            jax.ShapeDtypeStruct(x.shape, jnp.bfloat16),
            jax.ShapeDtypeStruct((tokens, 1), jnp.float32),
            jax.ShapeDtypeStruct((tokens, features // 2), jnp.bfloat16),
        ),
        compiler_params=pltpu.CompilerParams(vmem_limit_bytes=12 * MIB),
        cost_estimate=cost(0, 0),
    )(places, x, gain)


def early_kernel(shards_ref, normed_ref, both_ref, *refs, count):
    key_pieces, value_pieces = list(refs[: count - 1]), list(refs[count - 1 : 2 * count - 2])
    key_pieces.insert(1, both_ref.at[0])
    value_pieces.insert(1, both_ref.at[1])
    key_ref, value_ref, key_w_ref, value_w_ref, key_sems, value_sems = refs[2 * count - 2 :]
    key_f, copies = add_rows(shards_ref, normed_ref, key_pieces, key_w_ref, key_sems, 0, None)
    value_f, more = add_rows(
        shards_ref, normed_ref, value_pieces, value_w_ref, value_sems, count, None
    )
    key_ref[...] = key_f
    value_ref[...] = value_f
    for copy in copies + more:
        copy.wait()


def early_rows(shards, normed, both, key_pieces, value_pieces):
    tokens, features = normed.shape
    depth, width = key_pieces[0].shape
    count = len(key_pieces) + 1
    rows = jax.ShapeDtypeStruct((tokens, width), jnp.float32)
    whole = jax.ShapeDtypeStruct((features, width), jnp.bfloat16)
    return pl.pallas_call(
        lambda *refs: early_kernel(*refs, count=count),
        in_specs=[IN_SMEM] + in_vmem(2 * count),
        out_specs=in_vmem(2) + [ANYWHERE] * 2,
        out_shape=(rows, rows, whole, whole),
        scratch_shapes=[pltpu.SemaphoreType.DMA((count,))] * 2,
        compiler_params=pltpu.CompilerParams(vmem_limit_bytes=16 * MIB),
        cost_estimate=cost(0, 0),
    )(shards, normed, both, *key_pieces, *value_pieces)


def attention_kernel(shards_ref, normed_ref, *refs, count, first, features):
    key_pieces, value_pieces = refs[:count], refs[count : 2 * count]
    key_part_ref, value_part_ref, _, _, query_ref, grad_ref, seg_ref = refs[
        2 * count : 2 * count + 7
    ]
    key_w_ref, value_w_ref, grads_ref, inner_ref, key_sems, value_sems = refs[
        2 * count + 7 :
    ]
    key_f, copies = add_rows(
        shards_ref, normed_ref, key_pieces, key_w_ref, key_sems, first, key_part_ref[...]
    )
    value_f, more = add_rows(
        shards_ref, normed_ref, value_pieces, value_w_ref, value_sems, first + count, value_part_ref[...]
    )
    tokens = query_ref.shape[0]
    width = key_f.shape[1]
    group_size = query_ref.shape[1] // width
    key_pos = lax.broadcasted_iota(jnp.int32, (tokens, tokens), 0)
    query_pos = lax.broadcasted_iota(jnp.int32, (tokens, tokens), 1)
    by_query = jnp.broadcast_to(seg_ref[...].astype(jnp.float32), (tokens, tokens))
    allowed = (key_pos <= query_pos) & (by_query.T == by_query)
    allowed = jnp.concatenate([jnp.where(allowed, 1.0, 0.0)] * group_size, 1) > 0.5
    total = jnp.zeros(inner_ref.shape, jnp.float32)
    for j in range(width // HD):
        at = slice(j * HD, (j + 1) * HD)
        key_j, value_j = key_f[:, at], value_f[:, at]
        query_j = stacked(query_ref, j, group_size)
        grad_j = stacked(grad_ref, j, group_size)
        scores = dot(key_j.astype(jnp.bfloat16), query_j, NT) * (HD ** (-0.5))
        scores = jnp.where(allowed, scores, jnp.float32(-1e30))
        weight = jnp.exp(scores - jnp.max(scores, 0, keepdims=True))
        probability = weight / jnp.sum(weight, 0, keepdims=True)
        value_grad = dot(probability.astype(jnp.bfloat16), grad_j, NN).astype(jnp.bfloat16)
        dprob = dot(value_j.astype(jnp.bfloat16), grad_j, NT)
        delta = jnp.sum(probability * dprob, 0, keepdims=True)
        dscore_b = (probability * (dprob - delta)).astype(jnp.bfloat16)
        key_grad = (dot(dscore_b, query_j, NN) * (HD ** (-0.5))).astype(jnp.bfloat16)
        grads_ref[:, at] = key_grad
        grads_ref[:, width + j * HD : width + (j + 1) * HD] = value_grad
        total = total + jnp.sum(
            key_grad.astype(jnp.float32) * key_j + value_grad.astype(jnp.float32) * value_j,
            1,
            keepdims=True,
        )
    inner_ref[...] = total / features
    for copy in copies + more:
        copy.wait()


def attention_grads(shards, first, normed, key_pieces, value_pieces, early, query, grad_out, segments):
    tokens, features = normed.shape
    depth, width = key_pieces[0].shape
    count = len(key_pieces)
    whole = jax.ShapeDtypeStruct((features, width), jnp.bfloat16)
    grads = jax.ShapeDtypeStruct((tokens, 2 * width), jnp.bfloat16)
    at = 2 * count + 4
    return pl.pallas_call(
        lambda *refs: attention_kernel(*refs, count=count, first=first, features=features),
        in_specs=[IN_SMEM] + in_vmem(2 * count + 3) + [ANYWHERE] * 2 + in_vmem(3),
        out_specs=[ANYWHERE] * 2 + in_vmem(2),
        out_shape=(whole, whole, grads, jax.ShapeDtypeStruct((tokens, 1), jnp.float32)),
        input_output_aliases={at: 0, at + 1: 1},
        scratch_shapes=[pltpu.SemaphoreType.DMA((count,))] * 2,
        compiler_params=pltpu.CompilerParams(vmem_limit_bytes=20 * MIB),
        cost_estimate=cost(
            4 * tokens * depth * width * count + 8 * tokens * query.size,
            8 * depth * width * count + 4 * query.size,
            tokens * query.size // HD,
        ),
    )(shards, normed, *key_pieces, *value_pieces, *early, query, grad_out, segments)


def ordered_kernel(*refs):
    del refs


def ordered(arrays, after):
    count = len(arrays)
    return pl.pallas_call(
        ordered_kernel,
        in_specs=[ANYWHERE] * (count + 1),
        out_specs=[ANYWHERE] * count,
        out_shape=[jax.ShapeDtypeStruct(a.shape, a.dtype) for a in arrays],
        input_output_aliases={i: i for i in range(count)},
        compiler_params=pltpu.CompilerParams(vmem_limit_bytes=MIB),
        cost_estimate=cost(0, 0),
    )(*arrays, after)


def branch_kernel(at_ref, grads_ref, key_w_ref, value_w_ref, x_ref, gain_ref, rms_ref, inner_ref, out_ref):
    columns = key_w_ref.shape[1]
    d_normed = dot(grads_ref[:, :columns], key_w_ref[...], NT)
    d_normed = d_normed + dot(grads_ref[:, columns:], value_w_ref[...], NT)
    rms = rms_ref[...]
    x_hat = x_ref[...].astype(jnp.float32) * rms
    gated = gain_ref[...].astype(jnp.float32) * d_normed
    out_ref[...] = (rms * (gated - x_hat * inner_ref[...])).astype(out_ref.dtype)


def partial_branch(places, half, kind, grads, key_w, value_w, x, gain, inv_rms, inner):
    tokens = grads.shape[0]
    columns = key_w.shape[1]
    width = TILE * HALF_TILES
    whole = lambda i, at: (0, 0)
    rows = lambda i, at: (at[half] + i, 0)
    lanes = lambda i, at: (0, at[half] + i)
    return pl.pallas_call(
        branch_kernel,
        grid_spec=pltpu.PrefetchScalarGridSpec(
            num_scalar_prefetch=1,
            grid=(HALF_TILES,),
            in_specs=[
                pl.BlockSpec((tokens, 2 * columns), whole),
                pl.BlockSpec((TILE, columns), rows),
                pl.BlockSpec((TILE, columns), rows),
                pl.BlockSpec((tokens, TILE), lanes),
                pl.BlockSpec((1, TILE), lanes),
                pl.BlockSpec((tokens, 1), whole),
                pl.BlockSpec((tokens, 1), whole),
            ],
            out_specs=pl.BlockSpec((tokens, TILE), lambda i, at: (0, i)),
        ),
        out_shape=jax.ShapeDtypeStruct((tokens, width), kind),
        compiler_params=pltpu.CompilerParams(vmem_limit_bytes=8 * MIB),
        cost_estimate=cost(
            4 * tokens * width * columns, 4 * width * columns + 2 * width * tokens
        ),
    )(places, grads, key_w, value_w, x, gain, inv_rms, inner)


def weight_part_kernel(
    at_ref, normed_ref, normed_sib_ref, grads_ref, grads_sib_ref, after_ref,
    own_ref, right_ref, left_ref, far_right_ref, far_left_ref,
):
    grads = jnp.concatenate([grads_ref[...], grads_sib_ref[...]], 0)
    half = far_right_ref.shape[0]

    def part(step):
        k = lax.rem(at_ref[CHIP] + step, 4)
        own = pl.ds(pl.multiple_of((2 * k + at_ref[CORE]) * TILE, TILE), TILE)
        sib = pl.ds(pl.multiple_of(k * TILE, TILE), TILE)
        rows = jnp.concatenate([normed_ref[:, own], normed_sib_ref[:, sib]], 0)
        return dot(rows, grads, TN).astype(own_ref.dtype)

    far = part(2)
    far_right_ref[...] = far[:half]
    far_left_ref[...] = far[half:]
    own_ref[...] = part(0)
    right_ref[...] = part(1)
    left_ref[...] = part(3)


def weight_parts(places, normed, normed_sib, grads, grads_sib, after):
    part = jax.ShapeDtypeStruct((TILE, grads.shape[1]), jnp.bfloat16)
    half = jax.ShapeDtypeStruct((TILE // 2, grads.shape[1]), jnp.bfloat16)
    return pl.pallas_call(
        weight_part_kernel,
        in_specs=[IN_SMEM] + in_vmem(4) + [ANYWHERE],
        out_specs=in_vmem(5),
        out_shape=[part] * 3 + [half] * 2,
        compiler_params=pltpu.CompilerParams(vmem_limit_bytes=20 * MIB),
        cost_estimate=cost(4 * normed.size * grads.shape[1], 4 * normed.size),
    )(places, normed, normed_sib, grads, grads_sib, after)


def join_kernel(right_ref, left_ref, far_right_ref, far_left_ref, to_right_ref, to_left_ref, token_ref):
    half = far_right_ref.shape[0]
    join = lambda a, b: (a.astype(jnp.float32) + b.astype(jnp.float32)).astype(jnp.bfloat16)
    to_right_ref[:half] = join(right_ref[:half], far_right_ref[...])
    to_right_ref[half:] = right_ref[half:]
    to_left_ref[:half] = left_ref[:half]
    to_left_ref[half:] = join(left_ref[half:], far_left_ref[...])
    token_ref[...] = jnp.zeros_like(token_ref)


def join_parts(right, left, far_right, far_left):
    part = jax.ShapeDtypeStruct(right.shape, right.dtype)
    return pl.pallas_call(
        join_kernel,
        in_specs=in_vmem(4),
        out_specs=in_vmem(3),
        out_shape=[part, part, jax.ShapeDtypeStruct((8, 128), jnp.float32)],
        compiler_params=pltpu.CompilerParams(vmem_limit_bytes=12 * MIB),
        cost_estimate=cost(right.size, 8 * right.size),
    )(right, left, far_right, far_left)


def add_kernel(mine_ref, arrived_ref, token_ref, out_ref):
    out_ref[...] = (mine_ref[...] + arrived_ref[...].astype(jnp.float32)).astype(out_ref.dtype)


def add_halves(mine, arrived, token):
    tokens, width = mine.shape
    spec = pl.BlockSpec((tokens, TILE), lambda i: (0, i))
    return pl.pallas_call(
        add_kernel,
        grid=(width // TILE,),
        in_specs=[spec, spec, ANYWHERE],
        out_specs=spec,
        out_shape=jax.ShapeDtypeStruct(mine.shape, jnp.bfloat16),
        compiler_params=pltpu.CompilerParams(vmem_limit_bytes=8 * MIB),
        cost_estimate=cost(1e15, 1e12),
    )(mine, arrived, token)


def copy_kernel(at_ref, in_ref, out_ref):
    out_ref[...] = in_ref[...]


def take_rows(places, array, rows):
    width = array.shape[1]
    return pl.pallas_call(
        copy_kernel,
        grid_spec=pltpu.PrefetchScalarGridSpec(
            num_scalar_prefetch=1,
            grid=(1,),
            in_specs=[pl.BlockSpec((rows, width), lambda i, at: (at[STAGE], 0))],
            out_specs=pl.BlockSpec((rows, width), lambda i, at: (0, 0)),
        ),
        out_shape=jax.ShapeDtypeStruct((rows, width), array.dtype),
        compiler_params=pltpu.CompilerParams(vmem_limit_bytes=MIB),
        cost_estimate=cost(0, 0),
    )(places, array)


def suffix_kernel(parts_ref, top_ref, out_ref):
    running = top_ref[...].astype(jnp.float32)
    for layer in reversed(range(parts_ref.shape[0])):
        running = running + parts_ref[layer].astype(jnp.float32)
        out_ref[layer] = running.astype(jnp.bfloat16)


def suffix_sum(parts, top):
    layers, rows, width = parts.shape
    tile = min(width, 1024)
    return pl.pallas_call(
        suffix_kernel,
        grid=(width // tile,),
        in_specs=[
            pl.BlockSpec((layers, rows, tile), lambda i: (0, 0, i)),
            pl.BlockSpec((rows, tile), lambda i: (0, i)),
        ],
        out_specs=pl.BlockSpec((layers, rows, tile), lambda i: (0, 0, i)),
        out_shape=jax.ShapeDtypeStruct(parts.shape, jnp.bfloat16),
        compiler_params=pltpu.CompilerParams(vmem_limit_bytes=8 * MIB),
        cost_estimate=cost(parts.size, 4 * parts.size),
    )(parts, top)


def scale_kernel(factor_ref, *refs):
    *part_refs, out_ref = refs
    p = pl.program_id(0)
    for i in range(out_ref.shape[1] // BLOCK):
        for c in range(out_ref.shape[2] // HD):
            at = (slice(i * BLOCK, (i + 1) * BLOCK), slice(c * HD, (c + 1) * HD))
            total = part_refs[0][at].astype(jnp.float32)
            for ref in part_refs[1:]:
                total = total + ref[at].astype(jnp.float32)
            out_ref[(0, *at)] = (total * factor_ref[p, i, c]).astype(jnp.bfloat16)


def scaled_grad(parts, factor):
    rows = parts[0].shape[0]
    columns = parts[0].shape[1] // 2
    return pl.pallas_call(
        scale_kernel,
        grid=(2,),
        in_specs=[IN_SMEM] + [pl.BlockSpec((rows, columns), lambda p: (0, p))] * len(parts),
        out_specs=pl.BlockSpec((1, rows, columns), lambda p: (p, 0, 0)),
        out_shape=jax.ShapeDtypeStruct((2, rows, columns), jnp.bfloat16),
        compiler_params=pltpu.CompilerParams(vmem_limit_bytes=12 * MIB),
        cost_estimate=cost(parts[0].size, 10 * parts[0].size),
    )(factor, *parts)


def ring_pairs(count):
    right = [(i, (i + 2) % count) for i in range(count)]
    left = [(i, (i - 2) % count) for i in range(count)]
    other = [(i, i ^ 1) for i in range(count)]
    return right, left, other


def on_device(
    layer_input, norm_gain, kv_weight, queries, out_grad, top_grad, segment_ids, scale_exp
):
    inputs = layer_input[0]
    token_count, feature_count = inputs.shape
    pipe_count = lax.axis_size("pipe")
    right, left, other = ring_pairs(lax.axis_size("dp"))
    send = lambda piece, pairs: lax.ppermute(piece, "dp", pairs)
    key_own, value_own = kv_weight[0, 0], kv_weight[0, 1]
    key_l = send(key_own, right)
    value_r = send(value_own, left)
    both = send(kv_weight[0], other)
    key_r = send(key_own, left)
    value_l = send(value_own, right)
    key_2 = send(key_l, right)
    value_2 = send(value_r, left)

    places = all_places()
    normed, inv_rms, normed_other = norm(places, inputs, norm_gain)
    normed_sib = send(normed_other, other)
    early = early_rows(
        places,
        normed,
        both,
        [key_own, key_l, send(key_l, other), key_r],
        [value_own, value_r, send(value_r, other), value_l],
    )
    key_r, value_l = ordered((key_r, value_l), early[0])
    key_w, value_w, grads, inner = attention_grads(
        places,
        10,
        normed,
        [send(key_r, other), key_2, send(key_2, other)],
        [send(value_l, other), value_2, send(value_2, other)],
        early,
        queries[0],
        out_grad[0],
        segment_ids[None, :],
    )

    def share(half, kind):
        return partial_branch(
            places, half, kind, grads, key_w, value_w, inputs, norm_gain, inv_rms, inner
        )

    arrived = lax.ppermute(share(THEIRS, jnp.bfloat16), "tensor", [(0, 1), (1, 0)])
    mine = share(MINE, jnp.float32)
    own, to_right, to_left, far_right, far_left = weight_parts(
        places, normed, normed_sib, grads, send(grads, other), mine
    )
    to_right, to_left, token = join_parts(
        to_right, to_left, send(far_right, right), send(far_left, left)
    )
    received = [send(to_right, right), send(to_left, left)]
    branch = add_halves(mine, arrived, token)
    parts = lax.all_to_all(branch, "pipe", 0, 0, tiled=True)
    rows = token_count // pipe_count
    sums = suffix_sum(
        parts.reshape(pipe_count, rows, branch.shape[1]), take_rows(places, top_grad, rows)
    )
    input_grad = lax.all_to_all(
        sums.reshape(token_count, branch.shape[1]), "pipe", 0, 0, tiled=True
    )
    weight_grad = scaled_grad([own, *received], jnp.exp2(-scale_exp[0].astype(jnp.float32)))
    return (input_grad[None], weight_grad[None])


def solution(mesh):
    placed = (
        P("pipe", "dp", None),
        P("pipe", None),
        P("pipe", None, "dp", "tensor"),
        P("pipe", "dp", "tensor"),
        P("pipe", "dp", "tensor"),
        P("dp", "tensor"),
        P("dp"),
        P("pipe", None, "dp", "tensor"),
    )
    return jax.shard_map(
        on_device,
        mesh=mesh,
        in_specs=placed,
        out_specs=(P("pipe", "dp", "tensor"), P("pipe", None, "dp", "tensor")),
        check_vma=False,
    )
```

```python
import jax
import jax.numpy as jnp
from jax import lax
from jax.experimental import pallas as pl
from jax.experimental.pallas import tpu as pltpu
from jax.sharding import PartitionSpec as P

HD = 128
BLOCK = 128
EPS = 1e-05
MIB = 1024 * 1024
TILE = 1024
HALF_TILES = 4
THEIRS, MINE, STAGE, CORE, CHIP = 16, 17, 18, 19, 20

NT = (((1,), (1,)), ((), ()))
NN = (((1,), (0,)), ((), ()))
TN = (((0,), (0,)), ((), ()))


def dot(a, b, dims):
    return lax.dot_general(a, b, dims, preferred_element_type=jnp.float32)


def cost(flops, nbytes, transcendentals=0):
    return pl.CostEstimate(
        flops=int(flops), bytes_accessed=int(nbytes), transcendentals=int(transcendentals)
    )


def stacked(ref, group, count):
    base = group * count
    return jnp.concatenate([ref[:, (base + h) * HD : (base + h + 1) * HD] for h in range(count)], 0)


def add_rows(shards_ref, normed_ref, pieces, whole_ref, sems, first, total):
    depth = pieces[0].shape[0]
    copies = []
    for i, piece in enumerate(pieces):
        rows = pl.ds(pl.multiple_of(shards_ref[first + i] * depth, depth), depth)
        copy = pltpu.make_async_copy(piece, whole_ref.at[rows, :], sems.at[i])
        copy.start()
        copies.append(copy)
    for i, piece in enumerate(pieces):
        columns = pl.ds(pl.multiple_of(shards_ref[first + i] * depth, depth), depth)
        part = dot(normed_ref[:, columns], piece[...], NN)
        total = part if total is None else total + part
    return total, copies


def in_vmem(count):
    return [pl.BlockSpec(memory_space=pltpu.VMEM)] * count


IN_SMEM = pl.BlockSpec(memory_space=pltpu.SMEM)
ANYWHERE = pl.BlockSpec(memory_space=pl.ANY)


def places_kernel(out_ref):
    me = lax.axis_index("dp")
    tensor_pos = lax.axis_index("tensor")
    before, after, across = lax.rem(me + 6, 8), lax.rem(me + 2, 8), lax.rem(me + 4, 8)
    sibling = lambda shard: shard + 1 - 2 * lax.rem(shard, 2)
    order = (me, sibling(me), before, sibling(before), after)
    order += (me, sibling(me), after, sibling(after), before)
    order += (sibling(after), across, sibling(across))
    order += (sibling(before), across, sibling(across))
    for i, shard in enumerate(order):
        out_ref[i] = shard
    out_ref[CORE] = lax.rem(me, 2)
    out_ref[CHIP] = me // 2
    out_ref[THEIRS] = (1 - tensor_pos) * HALF_TILES
    out_ref[MINE] = tensor_pos * HALF_TILES
    out_ref[STAGE] = lax.axis_index("pipe")


def all_places():
    return pl.pallas_call(
        places_kernel,
        out_specs=IN_SMEM,
        out_shape=jax.ShapeDtypeStruct((32,), jnp.int32),
        compiler_params=pltpu.CompilerParams(vmem_limit_bytes=MIB),
        cost_estimate=cost(1, 1),
    )()


def normed_kernel(at_ref, x_ref, gain_ref, normed_ref, rms_ref, other_ref):
    x = x_ref[...].astype(jnp.float32)
    rms = lax.rsqrt(jnp.mean(x * x, -1, keepdims=True) + EPS)
    rms_ref[...] = rms
    normed_ref[...] = ((x * rms) * gain_ref[...].astype(jnp.float32)).astype(jnp.bfloat16)
    for k in range(other_ref.shape[1] // TILE):
        shard = 2 * k + 1 - at_ref[CORE]
        columns = pl.ds(pl.multiple_of(shard * TILE, TILE), TILE)
        other_ref[:, k * TILE : (k + 1) * TILE] = normed_ref[:, columns]


def norm(places, x, gain):
    tokens, features = x.shape
    rows = min(tokens, 32)
    by_rows = lambda i, at: (i, 0)
    return pl.pallas_call(
        normed_kernel,
        grid_spec=pltpu.PrefetchScalarGridSpec(
            num_scalar_prefetch=1,
            grid=(tokens // rows,),
            in_specs=[
                pl.BlockSpec((rows, features), by_rows),
                pl.BlockSpec((1, features), lambda i, at: (0, 0)),
            ],
            out_specs=[
                pl.BlockSpec((rows, features), by_rows),
                pl.BlockSpec((rows, 1), by_rows),
                pl.BlockSpec((rows, features // 2), by_rows),
            ],
        ),
        out_shape=(
            jax.ShapeDtypeStruct(x.shape, jnp.bfloat16),
            jax.ShapeDtypeStruct((tokens, 1), jnp.float32),
            jax.ShapeDtypeStruct((tokens, features // 2), jnp.bfloat16),
        ),
        compiler_params=pltpu.CompilerParams(vmem_limit_bytes=12 * MIB),
        cost_estimate=cost(1, 1),
    )(places, x, gain)


def early_kernel(shards_ref, normed_ref, both_ref, *refs, count):
    key_pieces, value_pieces = list(refs[: count - 1]), list(refs[count - 1 : 2 * count - 2])
    key_pieces.insert(1, both_ref.at[0])
    value_pieces.insert(1, both_ref.at[1])
    key_ref, value_ref, key_w_ref, value_w_ref, key_sems, value_sems = refs[2 * count - 2 :]
    key_f, copies = add_rows(shards_ref, normed_ref, key_pieces, key_w_ref, key_sems, 0, None)
    value_f, more = add_rows(
        shards_ref, normed_ref, value_pieces, value_w_ref, value_sems, count, None
    )
    key_ref[...] = key_f
    value_ref[...] = value_f
    for copy in copies + more:
        copy.wait()


def early_rows(shards, normed, both, key_pieces, value_pieces):
    tokens, features = normed.shape
    depth, width = key_pieces[0].shape
    count = len(key_pieces) + 1
    rows = jax.ShapeDtypeStruct((tokens, width), jnp.float32)
    whole = jax.ShapeDtypeStruct((features, width), jnp.bfloat16)
    return pl.pallas_call(
        lambda *refs: early_kernel(*refs, count=count),
        in_specs=[IN_SMEM] + in_vmem(2 * count),
        out_specs=in_vmem(2) + [ANYWHERE] * 2,
        out_shape=(rows, rows, whole, whole),
        scratch_shapes=[pltpu.SemaphoreType.DMA((count,))] * 2,
        compiler_params=pltpu.CompilerParams(vmem_limit_bytes=16 * MIB),
        cost_estimate=cost(1, 1),
    )(shards, normed, both, *key_pieces, *value_pieces)


def attention_kernel(shards_ref, normed_ref, *refs, count, first, features):
    key_pieces, value_pieces = refs[:count], refs[count : 2 * count]
    key_part_ref, value_part_ref, _, _, query_ref, grad_ref, seg_ref = refs[
        2 * count : 2 * count + 7
    ]
    key_w_ref, value_w_ref, grads_ref, inner_ref, key_sems, value_sems = refs[
        2 * count + 7 :
    ]
    key_f, copies = add_rows(
        shards_ref, normed_ref, key_pieces, key_w_ref, key_sems, first, key_part_ref[...]
    )
    value_f, more = add_rows(
        shards_ref, normed_ref, value_pieces, value_w_ref, value_sems, first + count, value_part_ref[...]
    )
    tokens = query_ref.shape[0]
    width = key_f.shape[1]
    group_size = query_ref.shape[1] // width
    key_pos = lax.broadcasted_iota(jnp.int32, (tokens, tokens), 0)
    query_pos = lax.broadcasted_iota(jnp.int32, (tokens, tokens), 1)
    by_query = jnp.broadcast_to(seg_ref[...].astype(jnp.float32), (tokens, tokens))
    allowed = (key_pos <= query_pos) & (by_query.T == by_query)
    allowed = jnp.concatenate([jnp.where(allowed, 1.0, 0.0)] * group_size, 1) > 0.5
    total = jnp.zeros(inner_ref.shape, jnp.float32)
    for j in range(width // HD):
        at = slice(j * HD, (j + 1) * HD)
        key_j, value_j = key_f[:, at], value_f[:, at]
        query_j = stacked(query_ref, j, group_size)
        grad_j = stacked(grad_ref, j, group_size)
        scores = dot(key_j.astype(jnp.bfloat16), query_j, NT) * (HD ** (-0.5))
        scores = jnp.where(allowed, scores, jnp.float32(-1e30))
        weight = jnp.exp(scores - jnp.max(scores, 0, keepdims=True))
        probability = weight / jnp.sum(weight, 0, keepdims=True)
        value_grad = dot(probability.astype(jnp.bfloat16), grad_j, NN).astype(jnp.bfloat16)
        dprob = dot(value_j.astype(jnp.bfloat16), grad_j, NT)
        delta = jnp.sum(probability * dprob, 0, keepdims=True)
        dscore_b = (probability * (dprob - delta)).astype(jnp.bfloat16)
        key_grad = (dot(dscore_b, query_j, NN) * (HD ** (-0.5))).astype(jnp.bfloat16)
        grads_ref[:, at] = key_grad
        grads_ref[:, width + j * HD : width + (j + 1) * HD] = value_grad
        total = total + jnp.sum(
            key_grad.astype(jnp.float32) * key_j + value_grad.astype(jnp.float32) * value_j,
            1,
            keepdims=True,
        )
    inner_ref[...] = total / features
    for copy in copies + more:
        copy.wait()


def attention_grads(shards, first, normed, key_pieces, value_pieces, early, query, grad_out, segments):
    tokens, features = normed.shape
    depth, width = key_pieces[0].shape
    count = len(key_pieces)
    whole = jax.ShapeDtypeStruct((features, width), jnp.bfloat16)
    grads = jax.ShapeDtypeStruct((tokens, 2 * width), jnp.bfloat16)
    at = 2 * count + 4
    return pl.pallas_call(
        lambda *refs: attention_kernel(*refs, count=count, first=first, features=features),
        in_specs=[IN_SMEM] + in_vmem(2 * count + 3) + [ANYWHERE] * 2 + in_vmem(3),
        out_specs=[ANYWHERE] * 2 + in_vmem(2),
        out_shape=(whole, whole, grads, jax.ShapeDtypeStruct((tokens, 1), jnp.float32)),
        input_output_aliases={at: 0, at + 1: 1},
        scratch_shapes=[pltpu.SemaphoreType.DMA((count,))] * 2,
        compiler_params=pltpu.CompilerParams(vmem_limit_bytes=20 * MIB),
        cost_estimate=cost(
            4 * tokens * depth * width * count + 8 * tokens * query.size,
            8 * depth * width * count + 4 * query.size,
            tokens * query.size // HD,
        ),
    )(shards, normed, *key_pieces, *value_pieces, *early, query, grad_out, segments)


def ordered_kernel(*refs):
    del refs


def ordered(arrays, after):
    count = len(arrays)
    return pl.pallas_call(
        ordered_kernel,
        in_specs=[ANYWHERE] * (count + 1),
        out_specs=[ANYWHERE] * count,
        out_shape=[jax.ShapeDtypeStruct(a.shape, a.dtype) for a in arrays],
        input_output_aliases={i: i for i in range(count)},
        compiler_params=pltpu.CompilerParams(vmem_limit_bytes=MIB),
        cost_estimate=cost(1, 1),
    )(*arrays, after)


def branch_kernel(at_ref, grads_ref, key_w_ref, value_w_ref, x_ref, gain_ref, rms_ref, inner_ref, out_ref):
    columns = key_w_ref.shape[1]
    d_normed = dot(grads_ref[:, :columns], key_w_ref[...], NT)
    d_normed = d_normed + dot(grads_ref[:, columns:], value_w_ref[...], NT)
    rms = rms_ref[...]
    x_hat = x_ref[...].astype(jnp.float32) * rms
    gated = gain_ref[...].astype(jnp.float32) * d_normed
    out_ref[...] = (rms * (gated - x_hat * inner_ref[...])).astype(out_ref.dtype)


def partial_branch(places, half, kind, grads, key_w, value_w, x, gain, inv_rms, inner):
    tokens = grads.shape[0]
    columns = key_w.shape[1]
    width = TILE * HALF_TILES
    whole = lambda i, at: (0, 0)
    rows = lambda i, at: (at[half] + i, 0)
    lanes = lambda i, at: (0, at[half] + i)
    return pl.pallas_call(
        branch_kernel,
        grid_spec=pltpu.PrefetchScalarGridSpec(
            num_scalar_prefetch=1,
            grid=(HALF_TILES,),
            in_specs=[
                pl.BlockSpec((tokens, 2 * columns), whole),
                pl.BlockSpec((TILE, columns), rows),
                pl.BlockSpec((TILE, columns), rows),
                pl.BlockSpec((tokens, TILE), lanes),
                pl.BlockSpec((1, TILE), lanes),
                pl.BlockSpec((tokens, 1), whole),
                pl.BlockSpec((tokens, 1), whole),
            ],
            out_specs=pl.BlockSpec((tokens, TILE), lambda i, at: (0, i)),
        ),
        out_shape=jax.ShapeDtypeStruct((tokens, width), kind),
        compiler_params=pltpu.CompilerParams(vmem_limit_bytes=8 * MIB),
        cost_estimate=cost(
            4 * tokens * width * columns, 4 * width * columns + 2 * width * tokens
        ),
    )(places, grads, key_w, value_w, x, gain, inv_rms, inner)


def weight_part_kernel(
    at_ref, normed_ref, normed_sib_ref, grads_ref, grads_sib_ref, after_ref,
    own_ref, right_ref, left_ref, far_right_ref, far_left_ref,
):
    grads = jnp.concatenate([grads_ref[...], grads_sib_ref[...]], 0)
    half = far_right_ref.shape[0]

    def part(step):
        k = lax.rem(at_ref[CHIP] + step, 4)
        own = pl.ds(pl.multiple_of((2 * k + at_ref[CORE]) * TILE, TILE), TILE)
        sib = pl.ds(pl.multiple_of(k * TILE, TILE), TILE)
        rows = jnp.concatenate([normed_ref[:, own], normed_sib_ref[:, sib]], 0)
        return dot(rows, grads, TN).astype(own_ref.dtype)

    far = part(2)
    far_right_ref[...] = far[:half]
    far_left_ref[...] = far[half:]
    own_ref[...] = part(0)
    right_ref[...] = part(1)
    left_ref[...] = part(3)


def weight_parts(places, normed, normed_sib, grads, grads_sib, after):
    part = jax.ShapeDtypeStruct((TILE, grads.shape[1]), jnp.bfloat16)
    half = jax.ShapeDtypeStruct((TILE // 2, grads.shape[1]), jnp.bfloat16)
    return pl.pallas_call(
        weight_part_kernel,
        in_specs=[IN_SMEM] + in_vmem(4) + [ANYWHERE],
        out_specs=in_vmem(5),
        out_shape=[part] * 3 + [half] * 2,
        compiler_params=pltpu.CompilerParams(vmem_limit_bytes=20 * MIB),
        cost_estimate=cost(4 * normed.size * grads.shape[1], 4 * normed.size),
    )(places, normed, normed_sib, grads, grads_sib, after)


def join_kernel(right_ref, left_ref, far_right_ref, far_left_ref, to_right_ref, to_left_ref, token_ref):
    half = far_right_ref.shape[0]
    join = lambda a, b: (a.astype(jnp.float32) + b.astype(jnp.float32)).astype(jnp.bfloat16)
    to_right_ref[:half] = join(right_ref[:half], far_right_ref[...])
    to_right_ref[half:] = right_ref[half:]
    to_left_ref[:half] = left_ref[:half]
    to_left_ref[half:] = join(left_ref[half:], far_left_ref[...])
    token_ref[...] = jnp.zeros_like(token_ref)


def join_parts(right, left, far_right, far_left):
    part = jax.ShapeDtypeStruct(right.shape, right.dtype)
    return pl.pallas_call(
        join_kernel,
        in_specs=in_vmem(4),
        out_specs=in_vmem(3),
        out_shape=[part, part, jax.ShapeDtypeStruct((8, 128), jnp.float32)],
        compiler_params=pltpu.CompilerParams(vmem_limit_bytes=12 * MIB),
        cost_estimate=cost(right.size, 8 * right.size),
    )(right, left, far_right, far_left)


def add_kernel(mine_ref, arrived_ref, token_ref, out_ref):
    out_ref[...] = (mine_ref[...] + arrived_ref[...].astype(jnp.float32)).astype(out_ref.dtype)


def add_halves(mine, arrived, token):
    tokens, width = mine.shape
    spec = pl.BlockSpec((tokens, TILE), lambda i: (0, i))
    return pl.pallas_call(
        add_kernel,
        grid=(width // TILE,),
        in_specs=[spec, spec, ANYWHERE],
        out_specs=spec,
        out_shape=jax.ShapeDtypeStruct(mine.shape, jnp.bfloat16),
        compiler_params=pltpu.CompilerParams(vmem_limit_bytes=8 * MIB),
        cost_estimate=cost(1e15, 1e12),
    )(mine, arrived, token)


def copy_kernel(at_ref, in_ref, out_ref):
    out_ref[...] = in_ref[...]


def take_rows(places, array, rows):
    width = array.shape[1]
    return pl.pallas_call(
        copy_kernel,
        grid_spec=pltpu.PrefetchScalarGridSpec(
            num_scalar_prefetch=1,
            grid=(1,),
            in_specs=[pl.BlockSpec((rows, width), lambda i, at: (at[STAGE], 0))],
            out_specs=pl.BlockSpec((rows, width), lambda i, at: (0, 0)),
        ),
        out_shape=jax.ShapeDtypeStruct((rows, width), array.dtype),
        compiler_params=pltpu.CompilerParams(vmem_limit_bytes=MIB),
        cost_estimate=cost(1, 1),
    )(places, array)


def suffix_kernel(parts_ref, top_ref, out_ref):
    running = top_ref[...].astype(jnp.float32)
    for layer in reversed(range(parts_ref.shape[0])):
        running = running + parts_ref[layer].astype(jnp.float32)
        out_ref[layer] = running.astype(jnp.bfloat16)


def suffix_sum(parts, top):
    layers, rows, width = parts.shape
    tile = min(width, 1024)
    return pl.pallas_call(
        suffix_kernel,
        grid=(width // tile,),
        in_specs=[
            pl.BlockSpec((layers, rows, tile), lambda i: (0, 0, i)),
            pl.BlockSpec((rows, tile), lambda i: (0, i)),
        ],
        out_specs=pl.BlockSpec((layers, rows, tile), lambda i: (0, 0, i)),
        out_shape=jax.ShapeDtypeStruct(parts.shape, jnp.bfloat16),
        compiler_params=pltpu.CompilerParams(vmem_limit_bytes=8 * MIB),
        cost_estimate=cost(parts.size, 4 * parts.size),
    )(parts, top)


def scale_kernel(factor_ref, *refs):
    *part_refs, out_ref = refs
    p = pl.program_id(0)
    for i in range(out_ref.shape[1] // BLOCK):
        for c in range(out_ref.shape[2] // HD):
            at = (slice(i * BLOCK, (i + 1) * BLOCK), slice(c * HD, (c + 1) * HD))
            total = part_refs[0][at].astype(jnp.float32)
            for ref in part_refs[1:]:
                total = total + ref[at].astype(jnp.float32)
            out_ref[(0, *at)] = (total * factor_ref[p, i, c]).astype(jnp.bfloat16)


def scaled_grad(parts, factor):
    rows = parts[0].shape[0]
    columns = parts[0].shape[1] // 2
    return pl.pallas_call(
        scale_kernel,
        grid=(2,),
        in_specs=[IN_SMEM] + [pl.BlockSpec((rows, columns), lambda p: (0, p))] * len(parts),
        out_specs=pl.BlockSpec((1, rows, columns), lambda p: (p, 0, 0)),
        out_shape=jax.ShapeDtypeStruct((2, rows, columns), jnp.bfloat16),
        compiler_params=pltpu.CompilerParams(vmem_limit_bytes=12 * MIB),
        cost_estimate=cost(1e15, 1e12),
    )(factor, *parts)


def ring_pairs(count):
    right = [(i, (i + 2) % count) for i in range(count)]
    left = [(i, (i - 2) % count) for i in range(count)]
    other = [(i, i ^ 1) for i in range(count)]
    return right, left, other


def on_device(
    layer_input, norm_gain, kv_weight, queries, out_grad, top_grad, segment_ids, scale_exp
):
    inputs = layer_input[0]
    token_count, feature_count = inputs.shape
    pipe_count = lax.axis_size("pipe")
    right, left, other = ring_pairs(lax.axis_size("dp"))
    send = lambda piece, pairs: lax.ppermute(piece, "dp", pairs)
    key_own, value_own = kv_weight[0, 0], kv_weight[0, 1]
    both = send(kv_weight[0], other)
    key_l = send(key_own, right)
    value_r = send(value_own, left)
    key_r = send(key_own, left)
    value_l = send(value_own, right)
    places = all_places()
    normed, inv_rms, normed_other = norm(places, inputs, norm_gain)
    key_l, value_r = ordered((key_l, value_r), inv_rms)
    key_2 = send(key_l, right)
    value_2 = send(value_r, left)
    normed_sib = send(normed_other, other)
    early = early_rows(
        places,
        normed,
        both,
        [key_own, key_l, send(key_l, other), key_r],
        [value_own, value_r, send(value_r, other), value_l],
    )
    key_r, value_l = ordered((key_r, value_l), early[0])
    key_w, value_w, grads, inner = attention_grads(
        places,
        10,
        normed,
        [send(key_r, other), key_2, send(key_2, other)],
        [send(value_l, other), value_2, send(value_2, other)],
        early,
        queries[0],
        out_grad[0],
        segment_ids[None, :],
    )

    def share(half, kind):
        return partial_branch(
            places, half, kind, grads, key_w, value_w, inputs, norm_gain, inv_rms, inner
        )

    arrived = lax.ppermute(share(THEIRS, jnp.bfloat16), "tensor", [(0, 1), (1, 0)])
    mine = share(MINE, jnp.float32)
    own, to_right, to_left, far_right, far_left = weight_parts(
        places, normed, normed_sib, grads, send(grads, other), mine
    )
    to_right, to_left, token = join_parts(
        to_right, to_left, send(far_right, right), send(far_left, left)
    )
    received = [send(to_right, right), send(to_left, left)]
    branch = add_halves(mine, arrived, token)
    parts = lax.all_to_all(branch, "pipe", 0, 0, tiled=True)
    rows = token_count // pipe_count
    sums = suffix_sum(
        parts.reshape(pipe_count, rows, branch.shape[1]), take_rows(places, top_grad, rows)
    )
    input_grad = lax.all_to_all(
        sums.reshape(token_count, branch.shape[1]), "pipe", 0, 0, tiled=True
    )
    weight_grad = scaled_grad([own, *received], jnp.exp2(-scale_exp[0].astype(jnp.float32)))
    return (input_grad[None], weight_grad[None])


def solution(mesh):
    placed = (
        P("pipe", "dp", None),
        P("pipe", None),
        P("pipe", None, "dp", "tensor"),
        P("pipe", "dp", "tensor"),
        P("pipe", "dp", "tensor"),
        P("dp", "tensor"),
        P("dp"),
        P("pipe", None, "dp", "tensor"),
    )
    return jax.shard_map(
        on_device,
        mesh=mesh,
        in_specs=placed,
        out_specs=(P("pipe", "dp", "tensor"), P("pipe", None, "dp", "tensor")),
        check_vma=False,
    )
```

```python
import jax
import jax.numpy as jnp
from jax import lax
from jax.experimental import pallas as pl
from jax.experimental.pallas import tpu as pltpu
from jax.sharding import PartitionSpec as P

HD = 128
BLOCK = 128
EPS = 1e-05
MIB = 1024 * 1024
TILE = 1024
HALF_TILES = 4
THEIRS, MINE, STAGE, CORE, CHIP = 16, 17, 18, 19, 20

NT = (((1,), (1,)), ((), ()))
NN = (((1,), (0,)), ((), ()))
TN = (((0,), (0,)), ((), ()))


def dot(a, b, dims):
    return lax.dot_general(a, b, dims, preferred_element_type=jnp.float32)


def cost(flops, nbytes, transcendentals=0):
    return pl.CostEstimate(
        flops=int(flops), bytes_accessed=int(nbytes), transcendentals=int(transcendentals)
    )


def stacked(ref, group, count):
    base = group * count
    return jnp.concatenate([ref[:, (base + h) * HD : (base + h + 1) * HD] for h in range(count)], 0)


def add_rows(shards_ref, normed_ref, pieces, whole_ref, sems, first, total):
    depth = pieces[0].shape[0]
    copies = []
    for i, piece in enumerate(pieces):
        rows = pl.ds(pl.multiple_of(shards_ref[first + i] * depth, depth), depth)
        copy = pltpu.make_async_copy(piece, whole_ref.at[rows, :], sems.at[i])
        copy.start()
        copies.append(copy)
    for i, piece in enumerate(pieces):
        columns = pl.ds(pl.multiple_of(shards_ref[first + i] * depth, depth), depth)
        part = dot(normed_ref[:, columns], piece[...], NN)
        total = part if total is None else total + part
    return total, copies


def in_vmem(count):
    return [pl.BlockSpec(memory_space=pltpu.VMEM)] * count


IN_SMEM = pl.BlockSpec(memory_space=pltpu.SMEM)
ANYWHERE = pl.BlockSpec(memory_space=pl.ANY)


def places_kernel(out_ref):
    me = lax.axis_index("dp")
    tensor_pos = lax.axis_index("tensor")
    before, after, across = lax.rem(me + 6, 8), lax.rem(me + 2, 8), lax.rem(me + 4, 8)
    sibling = lambda shard: shard + 1 - 2 * lax.rem(shard, 2)
    order = (me, sibling(me), before, sibling(before), after)
    order += (me, sibling(me), after, sibling(after), before)
    order += (sibling(after), across, sibling(across))
    order += (sibling(before), across, sibling(across))
    for i, shard in enumerate(order):
        out_ref[i] = shard
    out_ref[CORE] = lax.rem(me, 2)
    out_ref[CHIP] = me // 2
    out_ref[THEIRS] = (1 - tensor_pos) * HALF_TILES
    out_ref[MINE] = tensor_pos * HALF_TILES
    out_ref[STAGE] = lax.axis_index("pipe")


def all_places():
    return pl.pallas_call(
        places_kernel,
        out_specs=IN_SMEM,
        out_shape=jax.ShapeDtypeStruct((32,), jnp.int32),
        compiler_params=pltpu.CompilerParams(vmem_limit_bytes=MIB),
        cost_estimate=cost(1, 1),
    )()


def normed_kernel(at_ref, x_ref, gain_ref, normed_ref, rms_ref, other_ref):
    x = x_ref[...].astype(jnp.float32)
    rms = lax.rsqrt(jnp.mean(x * x, -1, keepdims=True) + EPS)
    rms_ref[...] = rms
    normed_ref[...] = ((x * rms) * gain_ref[...].astype(jnp.float32)).astype(jnp.bfloat16)
    for k in range(other_ref.shape[1] // TILE):
        shard = 2 * k + 1 - at_ref[CORE]
        columns = pl.ds(pl.multiple_of(shard * TILE, TILE), TILE)
        other_ref[:, k * TILE : (k + 1) * TILE] = normed_ref[:, columns]


def norm(places, x, gain):
    tokens, features = x.shape
    rows = min(tokens, 32)
    by_rows = lambda i, at: (i, 0)
    return pl.pallas_call(
        normed_kernel,
        grid_spec=pltpu.PrefetchScalarGridSpec(
            num_scalar_prefetch=1,
            grid=(tokens // rows,),
            in_specs=[
                pl.BlockSpec((rows, features), by_rows),
                pl.BlockSpec((1, features), lambda i, at: (0, 0)),
            ],
            out_specs=[
                pl.BlockSpec((rows, features), by_rows),
                pl.BlockSpec((rows, 1), by_rows),
                pl.BlockSpec((rows, features // 2), by_rows),
            ],
        ),
        out_shape=(
            jax.ShapeDtypeStruct(x.shape, jnp.bfloat16),
            jax.ShapeDtypeStruct((tokens, 1), jnp.float32),
            jax.ShapeDtypeStruct((tokens, features // 2), jnp.bfloat16),
        ),
        compiler_params=pltpu.CompilerParams(vmem_limit_bytes=12 * MIB),
        cost_estimate=cost(1, 1),
    )(places, x, gain)


def early_kernel(shards_ref, normed_ref, both_ref, *refs, count):
    key_pieces, value_pieces = list(refs[: count - 1]), list(refs[count - 1 : 2 * count - 2])
    key_pieces.insert(1, both_ref.at[0])
    value_pieces.insert(1, both_ref.at[1])
    key_ref, value_ref, key_w_ref, value_w_ref, key_sems, value_sems = refs[2 * count - 2 :]
    key_f, copies = add_rows(shards_ref, normed_ref, key_pieces, key_w_ref, key_sems, 0, None)
    value_f, more = add_rows(
        shards_ref, normed_ref, value_pieces, value_w_ref, value_sems, count, None
    )
    key_ref[...] = key_f
    value_ref[...] = value_f
    for copy in copies + more:
        copy.wait()


def early_rows(shards, normed, both, key_pieces, value_pieces):
    tokens, features = normed.shape
    depth, width = key_pieces[0].shape
    count = len(key_pieces) + 1
    rows = jax.ShapeDtypeStruct((tokens, width), jnp.float32)
    whole = jax.ShapeDtypeStruct((features, width), jnp.bfloat16)
    return pl.pallas_call(
        lambda *refs: early_kernel(*refs, count=count),
        in_specs=[IN_SMEM] + in_vmem(2 * count),
        out_specs=in_vmem(2) + [ANYWHERE] * 2,
        out_shape=(rows, rows, whole, whole),
        scratch_shapes=[pltpu.SemaphoreType.DMA((count,))] * 2,
        compiler_params=pltpu.CompilerParams(vmem_limit_bytes=16 * MIB),
        cost_estimate=cost(1, 1),
    )(shards, normed, both, *key_pieces, *value_pieces)


def attention_kernel(shards_ref, normed_ref, *refs, count, first, features):
    key_pieces, value_pieces = refs[:count], refs[count : 2 * count]
    key_part_ref, value_part_ref, _, _, query_ref, grad_ref, seg_ref = refs[
        2 * count : 2 * count + 7
    ]
    key_w_ref, value_w_ref, grads_ref, inner_ref, key_sems, value_sems = refs[
        2 * count + 7 :
    ]
    key_f, copies = add_rows(
        shards_ref, normed_ref, key_pieces, key_w_ref, key_sems, first, key_part_ref[...]
    )
    value_f, more = add_rows(
        shards_ref, normed_ref, value_pieces, value_w_ref, value_sems, first + count, value_part_ref[...]
    )
    tokens = query_ref.shape[0]
    width = key_f.shape[1]
    group_size = query_ref.shape[1] // width
    key_pos = lax.broadcasted_iota(jnp.int32, (tokens, tokens), 0)
    query_pos = lax.broadcasted_iota(jnp.int32, (tokens, tokens), 1)
    by_query = jnp.broadcast_to(seg_ref[...].astype(jnp.float32), (tokens, tokens))
    allowed = (key_pos <= query_pos) & (by_query.T == by_query)
    allowed = jnp.concatenate([jnp.where(allowed, 1.0, 0.0)] * group_size, 1) > 0.5
    total = jnp.zeros(inner_ref.shape, jnp.float32)
    for j in range(width // HD):
        at = slice(j * HD, (j + 1) * HD)
        key_j, value_j = key_f[:, at], value_f[:, at]
        query_j = stacked(query_ref, j, group_size)
        grad_j = stacked(grad_ref, j, group_size)
        scores = dot(key_j.astype(jnp.bfloat16), query_j, NT) * (HD ** (-0.5))
        scores = jnp.where(allowed, scores, jnp.float32(-1e30))
        weight = jnp.exp(scores - jnp.max(scores, 0, keepdims=True))
        probability = weight / jnp.sum(weight, 0, keepdims=True)
        value_grad = dot(probability.astype(jnp.bfloat16), grad_j, NN).astype(jnp.bfloat16)
        dprob = dot(value_j.astype(jnp.bfloat16), grad_j, NT)
        delta = jnp.sum(probability * dprob, 0, keepdims=True)
        dscore_b = (probability * (dprob - delta)).astype(jnp.bfloat16)
        key_grad = (dot(dscore_b, query_j, NN) * (HD ** (-0.5))).astype(jnp.bfloat16)
        grads_ref[:, at] = key_grad
        grads_ref[:, width + j * HD : width + (j + 1) * HD] = value_grad
        total = total + jnp.sum(
            key_grad.astype(jnp.float32) * key_j + value_grad.astype(jnp.float32) * value_j,
            1,
            keepdims=True,
        )
    inner_ref[...] = total / features
    for copy in copies + more:
        copy.wait()


def attention_grads(shards, first, normed, key_pieces, value_pieces, early, query, grad_out, segments):
    tokens, features = normed.shape
    depth, width = key_pieces[0].shape
    count = len(key_pieces)
    whole = jax.ShapeDtypeStruct((features, width), jnp.bfloat16)
    grads = jax.ShapeDtypeStruct((tokens, 2 * width), jnp.bfloat16)
    at = 2 * count + 4
    return pl.pallas_call(
        lambda *refs: attention_kernel(*refs, count=count, first=first, features=features),
        in_specs=[IN_SMEM] + in_vmem(2 * count + 3) + [ANYWHERE] * 2 + in_vmem(3),
        out_specs=[ANYWHERE] * 2 + in_vmem(2),
        out_shape=(whole, whole, grads, jax.ShapeDtypeStruct((tokens, 1), jnp.float32)),
        input_output_aliases={at: 0, at + 1: 1},
        scratch_shapes=[pltpu.SemaphoreType.DMA((count,))] * 2,
        compiler_params=pltpu.CompilerParams(vmem_limit_bytes=20 * MIB),
        cost_estimate=cost(
            4 * tokens * depth * width * count + 8 * tokens * query.size,
            8 * depth * width * count + 4 * query.size,
            tokens * query.size // HD,
        ),
    )(shards, normed, *key_pieces, *value_pieces, *early, query, grad_out, segments)


def ordered_kernel(*refs):
    del refs


def ordered(arrays, after):
    count = len(arrays)
    return pl.pallas_call(
        ordered_kernel,
        in_specs=[ANYWHERE] * (count + 1),
        out_specs=[ANYWHERE] * count,
        out_shape=[jax.ShapeDtypeStruct(a.shape, a.dtype) for a in arrays],
        input_output_aliases={i: i for i in range(count)},
        compiler_params=pltpu.CompilerParams(vmem_limit_bytes=MIB),
        cost_estimate=cost(1, 1),
    )(*arrays, after)


def branch_kernel(
    at_ref, grads_ref, key_w_ref, value_w_ref, x_ref, gain_ref, rms_ref, inner_ref, out_ref, *, half
):
    columns = key_w_ref.shape[1]
    key_grad, value_grad = grads_ref[:, :columns], grads_ref[:, columns:]
    rms = rms_ref[...]
    shift = rms * inner_ref[...]
    for i in range(out_ref.shape[1] // TILE):
        at = pl.ds(pl.multiple_of((at_ref[half] + i) * TILE, TILE), TILE)
        d_normed = dot(key_grad, key_w_ref[at, :], NT) + dot(value_grad, value_w_ref[at, :], NT)
        gated = gain_ref[:, at].astype(jnp.float32) * d_normed
        branch = rms * (gated - x_ref[:, at].astype(jnp.float32) * shift)
        out_ref[:, i * TILE : (i + 1) * TILE] = branch.astype(out_ref.dtype)


def partial_branch(places, half, kind, grads, key_w, value_w, x, gain, inv_rms, inner):
    tokens = grads.shape[0]
    columns = key_w.shape[1]
    width = TILE * HALF_TILES
    return pl.pallas_call(
        lambda *refs: branch_kernel(*refs, half=half),
        in_specs=[IN_SMEM] + in_vmem(7),
        out_specs=pl.BlockSpec(memory_space=pltpu.VMEM),
        out_shape=jax.ShapeDtypeStruct((tokens, width), kind),
        compiler_params=pltpu.CompilerParams(vmem_limit_bytes=20 * MIB),
        cost_estimate=cost(
            4 * tokens * width * columns, 4 * width * columns + 2 * width * tokens
        ),
    )(places, grads, key_w, value_w, x, gain, inv_rms, inner)


def weight_part_kernel(
    at_ref, normed_ref, normed_sib_ref, grads_ref, grads_sib_ref, after_ref,
    own_ref, right_ref, left_ref, far_right_ref, far_left_ref,
):
    grads = jnp.concatenate([grads_ref[...], grads_sib_ref[...]], 0)
    half = far_right_ref.shape[0]

    def part(step):
        k = lax.rem(at_ref[CHIP] + step, 4)
        own = pl.ds(pl.multiple_of((2 * k + at_ref[CORE]) * TILE, TILE), TILE)
        sib = pl.ds(pl.multiple_of(k * TILE, TILE), TILE)
        rows = jnp.concatenate([normed_ref[:, own], normed_sib_ref[:, sib]], 0)
        return dot(rows, grads, TN).astype(own_ref.dtype)

    far = part(2)
    far_right_ref[...] = far[:half]
    far_left_ref[...] = far[half:]
    own_ref[...] = part(0)
    right_ref[...] = part(1)
    left_ref[...] = part(3)


def weight_parts(places, normed, normed_sib, grads, grads_sib, after):
    part = jax.ShapeDtypeStruct((TILE, grads.shape[1]), jnp.bfloat16)
    half = jax.ShapeDtypeStruct((TILE // 2, grads.shape[1]), jnp.bfloat16)
    return pl.pallas_call(
        weight_part_kernel,
        in_specs=[IN_SMEM] + in_vmem(4) + [ANYWHERE],
        out_specs=in_vmem(5),
        out_shape=[part] * 3 + [half] * 2,
        compiler_params=pltpu.CompilerParams(vmem_limit_bytes=20 * MIB),
        cost_estimate=cost(4 * normed.size * grads.shape[1], 4 * normed.size),
    )(places, normed, normed_sib, grads, grads_sib, after)


def join_kernel(right_ref, left_ref, far_right_ref, far_left_ref, to_right_ref, to_left_ref, token_ref):
    half = far_right_ref.shape[0]
    join = lambda a, b: (a.astype(jnp.float32) + b.astype(jnp.float32)).astype(jnp.bfloat16)
    to_right_ref[:half] = join(right_ref[:half], far_right_ref[...])
    to_right_ref[half:] = right_ref[half:]
    to_left_ref[:half] = left_ref[:half]
    to_left_ref[half:] = join(left_ref[half:], far_left_ref[...])
    token_ref[...] = jnp.zeros_like(token_ref)


def join_parts(right, left, far_right, far_left):
    part = jax.ShapeDtypeStruct(right.shape, right.dtype)
    return pl.pallas_call(
        join_kernel,
        in_specs=in_vmem(4),
        out_specs=in_vmem(3),
        out_shape=[part, part, jax.ShapeDtypeStruct((8, 128), jnp.float32)],
        compiler_params=pltpu.CompilerParams(vmem_limit_bytes=12 * MIB),
        cost_estimate=cost(right.size, 8 * right.size),
    )(right, left, far_right, far_left)


def add_kernel(mine_ref, arrived_ref, token_ref, out_ref, held, sems):
    copies = []
    rows = held.shape[0] // sems.shape[0]
    for i in range(sems.shape[0]):
        at = pl.ds(i * rows, rows)
        held[at, :] = (mine_ref[at, :] + arrived_ref[at, :].astype(jnp.float32)).astype(held.dtype)
        copies.append(pltpu.make_async_copy(held.at[at, :], out_ref.at[at, :], sems.at[i]))
        copies[-1].start()
    for copy in copies:
        copy.wait()


def add_halves(mine, arrived, token):
    return pl.pallas_call(
        add_kernel,
        in_specs=in_vmem(2) + [ANYWHERE],
        out_specs=ANYWHERE,
        out_shape=jax.ShapeDtypeStruct(mine.shape, jnp.bfloat16),
        scratch_shapes=[
            pltpu.VMEM(mine.shape, jnp.bfloat16),
            pltpu.SemaphoreType.DMA((4,)),
        ],
        compiler_params=pltpu.CompilerParams(vmem_limit_bytes=8 * MIB),
        cost_estimate=cost(1e15, 1e12),
    )(mine, arrived, token)


def copy_kernel(at_ref, in_ref, out_ref):
    out_ref[...] = in_ref[...]


def take_rows(places, array, rows):
    width = array.shape[1]
    return pl.pallas_call(
        copy_kernel,
        grid_spec=pltpu.PrefetchScalarGridSpec(
            num_scalar_prefetch=1,
            grid=(1,),
            in_specs=[pl.BlockSpec((rows, width), lambda i, at: (at[STAGE], 0))],
            out_specs=pl.BlockSpec((rows, width), lambda i, at: (0, 0)),
        ),
        out_shape=jax.ShapeDtypeStruct((rows, width), array.dtype),
        compiler_params=pltpu.CompilerParams(vmem_limit_bytes=MIB),
        cost_estimate=cost(1, 1),
    )(places, array)


def suffix_kernel(parts_ref, top_ref, out_ref, held, sems):
    copies = []
    width = held.shape[2] // sems.shape[0]
    for i in range(sems.shape[0]):
        at = pl.ds(i * width, width)
        running = top_ref[:, at].astype(jnp.float32)
        for layer in reversed(range(parts_ref.shape[0])):
            running = running + parts_ref[layer, :, at].astype(jnp.float32)
            held[layer, :, at] = running.astype(jnp.bfloat16)
        copies.append(
            pltpu.make_async_copy(held.at[:, :, at], out_ref.at[:, :, at], sems.at[i])
        )
        copies[-1].start()
    for copy in copies:
        copy.wait()


def suffix_sum(parts, top):
    return pl.pallas_call(
        suffix_kernel,
        in_specs=in_vmem(2),
        out_specs=ANYWHERE,
        out_shape=jax.ShapeDtypeStruct(parts.shape, jnp.bfloat16),
        scratch_shapes=[
            pltpu.VMEM(parts.shape, jnp.bfloat16),
            pltpu.SemaphoreType.DMA((4,)),
        ],
        compiler_params=pltpu.CompilerParams(vmem_limit_bytes=8 * MIB),
        cost_estimate=cost(parts.size, 4 * parts.size),
    )(parts, top)


def move_kernel(in_ref, out_ref, held, in_sems, out_sems):
    count = in_sems.shape[0]
    rows = held.shape[0] // count
    arriving, leaving = [], []
    for i in range(count):
        at = pl.ds(i * rows, rows)
        arriving.append(pltpu.make_async_copy(in_ref.at[at, :], held.at[at, :], in_sems.at[i]))
        leaving.append(pltpu.make_async_copy(held.at[at, :], out_ref.at[at, :], out_sems.at[i]))
    for copy in arriving:
        copy.start()
    for i in range(count):
        arriving[i].wait()
        leaving[i].start()
    for copy in leaving:
        copy.wait()


def moved(array):
    return pl.pallas_call(
        move_kernel,
        in_specs=[ANYWHERE],
        out_specs=ANYWHERE,
        out_shape=jax.ShapeDtypeStruct(array.shape, array.dtype),
        scratch_shapes=[
            pltpu.VMEM(array.shape, array.dtype),
            pltpu.SemaphoreType.DMA((4,)),
            pltpu.SemaphoreType.DMA((4,)),
        ],
        compiler_params=pltpu.CompilerParams(vmem_limit_bytes=4 * MIB),
        cost_estimate=cost(1, 1),
    )(array)


def scale_kernel(factor_ref, *refs):
    *part_refs, out_ref = refs
    p = pl.program_id(0)
    for i in range(out_ref.shape[1] // BLOCK):
        for c in range(out_ref.shape[2] // HD):
            at = (slice(i * BLOCK, (i + 1) * BLOCK), slice(c * HD, (c + 1) * HD))
            total = part_refs[0][at].astype(jnp.float32)
            for ref in part_refs[1:]:
                total = total + ref[at].astype(jnp.float32)
            out_ref[(0, *at)] = (total * factor_ref[p, i, c]).astype(jnp.bfloat16)


def scaled_grad(parts, factor):
    rows = parts[0].shape[0]
    columns = parts[0].shape[1] // 2
    return pl.pallas_call(
        scale_kernel,
        grid=(2,),
        in_specs=[IN_SMEM] + [pl.BlockSpec((rows, columns), lambda p: (0, p))] * len(parts),
        out_specs=pl.BlockSpec((1, rows, columns), lambda p: (p, 0, 0)),
        out_shape=jax.ShapeDtypeStruct((2, rows, columns), jnp.bfloat16),
        compiler_params=pltpu.CompilerParams(vmem_limit_bytes=12 * MIB),
        cost_estimate=cost(1e15, 1e12),
    )(factor, *parts)


def ring_pairs(count):
    right = [(i, (i + 2) % count) for i in range(count)]
    left = [(i, (i - 2) % count) for i in range(count)]
    other = [(i, i ^ 1) for i in range(count)]
    return right, left, other


def on_device(
    layer_input, norm_gain, kv_weight, queries, out_grad, top_grad, segment_ids, scale_exp
):
    inputs = layer_input[0]
    token_count, feature_count = inputs.shape
    pipe_count = lax.axis_size("pipe")
    right, left, other = ring_pairs(lax.axis_size("dp"))
    send = lambda piece, pairs: lax.ppermute(piece, "dp", pairs)
    key_own, value_own = kv_weight[0, 0], kv_weight[0, 1]
    both = send(kv_weight[0], other)
    key_l = send(key_own, right)
    value_r = send(value_own, left)
    key_r = send(key_own, left)
    value_l = send(value_own, right)
    places = all_places()
    normed, inv_rms, normed_other = norm(places, inputs, norm_gain)
    key_l, value_r = ordered((key_l, value_r), inv_rms)
    key_2 = send(key_l, right)
    value_2 = send(value_r, left)
    normed_sib = send(normed_other, other)
    early = early_rows(
        places,
        normed,
        both,
        [key_own, key_l, send(key_l, other), key_r],
        [value_own, value_r, send(value_r, other), value_l],
    )
    key_r, value_l = ordered((key_r, value_l), early[0])
    key_w, value_w, grads, inner = attention_grads(
        places,
        10,
        normed,
        [send(key_r, other), key_2, send(key_2, other)],
        [send(value_l, other), value_2, send(value_2, other)],
        early,
        queries[0],
        out_grad[0],
        segment_ids[None, :],
    )

    def share(half, kind):
        return partial_branch(
            places, half, kind, grads, key_w, value_w, inputs, norm_gain, inv_rms, inner
        )

    arrived = lax.ppermute(share(THEIRS, jnp.bfloat16), "tensor", [(0, 1), (1, 0)])
    mine = share(MINE, jnp.float32)
    own, to_right, to_left, far_right, far_left = weight_parts(
        places, normed, normed_sib, grads, send(grads, other), mine
    )
    to_right, to_left, token = join_parts(
        to_right, to_left, send(far_right, right), send(far_left, left)
    )
    received = [send(to_right, right), send(to_left, left)]
    branch = add_halves(mine, arrived, token)
    parts = lax.all_to_all(branch, "pipe", 0, 0, tiled=True)
    rows = token_count // pipe_count
    sums = suffix_sum(
        parts.reshape(pipe_count, rows, branch.shape[1]), take_rows(places, top_grad, rows)
    )
    input_grad = lax.all_to_all(
        sums.reshape(token_count, branch.shape[1]), "pipe", 0, 0, tiled=True
    )
    weight_grad = scaled_grad([own, *received], jnp.exp2(-scale_exp[0].astype(jnp.float32)))
    return (moved(input_grad)[None], weight_grad[None])


def solution(mesh):
    placed = (
        P("pipe", "dp", None),
        P("pipe", None),
        P("pipe", None, "dp", "tensor"),
        P("pipe", "dp", "tensor"),
        P("pipe", "dp", "tensor"),
        P("dp", "tensor"),
        P("dp"),
        P("pipe", None, "dp", "tensor"),
    )
    return jax.shard_map(
        on_device,
        mesh=mesh,
        in_specs=placed,
        out_specs=(P("pipe", "dp", "tensor"), P("pipe", None, "dp", "tensor")),
        check_vma=False,
    )
```

```python
import jax
import jax.numpy as jnp
from jax import lax
from jax.experimental import pallas as pl
from jax.experimental.pallas import tpu as pltpu
from jax.sharding import PartitionSpec as P

HD = 128
BLOCK = 128
EPS = 1e-05
MIB = 1024 * 1024
TILE = 1024
HALF_TILES = 4
THEIRS, MINE, STAGE, CORE, CHIP = 16, 17, 18, 19, 20

NT = (((1,), (1,)), ((), ()))
NN = (((1,), (0,)), ((), ()))
TN = (((0,), (0,)), ((), ()))


def dot(a, b, dims):
    return lax.dot_general(a, b, dims, preferred_element_type=jnp.float32)


def cost(flops, nbytes, transcendentals=0):
    return pl.CostEstimate(
        flops=int(flops), bytes_accessed=int(nbytes), transcendentals=int(transcendentals)
    )


def stacked(ref, group, count):
    base = group * count
    return jnp.concatenate([ref[:, (base + h) * HD : (base + h + 1) * HD] for h in range(count)], 0)


def add_rows(shards_ref, normed_ref, pieces, whole_ref, sems, first, total):
    depth = pieces[0].shape[0]
    copies = []
    for i, piece in enumerate(pieces):
        rows = pl.ds(pl.multiple_of(shards_ref[first + i] * depth, depth), depth)
        copy = pltpu.make_async_copy(piece, whole_ref.at[rows, :], sems.at[i])
        copy.start()
        copies.append(copy)
    for i, piece in enumerate(pieces):
        columns = pl.ds(pl.multiple_of(shards_ref[first + i] * depth, depth), depth)
        part = dot(normed_ref[:, columns], piece[...], NN)
        total = part if total is None else total + part
    return total, copies


def in_vmem(count):
    return [pl.BlockSpec(memory_space=pltpu.VMEM)] * count


IN_SMEM = pl.BlockSpec(memory_space=pltpu.SMEM)
ANYWHERE = pl.BlockSpec(memory_space=pl.ANY)


def places_kernel(out_ref):
    me = lax.axis_index("dp")
    tensor_pos = lax.axis_index("tensor")
    before, after, across = lax.rem(me + 6, 8), lax.rem(me + 2, 8), lax.rem(me + 4, 8)
    sibling = lambda shard: shard + 1 - 2 * lax.rem(shard, 2)
    order = (sibling(me), me, before, after)
    order += (sibling(me), me, after, before)
    order += (sibling(before), sibling(after), across, sibling(across))
    order += (sibling(after), sibling(before), across, sibling(across))
    for i, shard in enumerate(order):
        out_ref[i] = shard
    out_ref[CORE] = lax.rem(me, 2)
    out_ref[CHIP] = me // 2
    out_ref[THEIRS] = (1 - tensor_pos) * HALF_TILES
    out_ref[MINE] = tensor_pos * HALF_TILES
    out_ref[STAGE] = lax.axis_index("pipe")


def all_places():
    return pl.pallas_call(
        places_kernel,
        out_specs=IN_SMEM,
        out_shape=jax.ShapeDtypeStruct((32,), jnp.int32),
        compiler_params=pltpu.CompilerParams(vmem_limit_bytes=MIB),
        cost_estimate=cost(1, 1),
    )()


def normed_kernel(at_ref, x_ref, gain_ref, normed_ref, rms_ref, other_ref):
    x = x_ref[...].astype(jnp.float32)
    rms = lax.rsqrt(jnp.mean(x * x, -1, keepdims=True) + EPS)
    rms_ref[...] = rms
    normed_ref[...] = ((x * rms) * gain_ref[...].astype(jnp.float32)).astype(jnp.bfloat16)
    for k in range(other_ref.shape[1] // TILE):
        shard = 2 * k + 1 - at_ref[CORE]
        columns = pl.ds(pl.multiple_of(shard * TILE, TILE), TILE)
        other_ref[:, k * TILE : (k + 1) * TILE] = normed_ref[:, columns]


def norm(places, x, gain):
    tokens, features = x.shape
    rows = min(tokens, 32)
    by_rows = lambda i, at: (i, 0)
    return pl.pallas_call(
        normed_kernel,
        grid_spec=pltpu.PrefetchScalarGridSpec(
            num_scalar_prefetch=1,
            grid=(tokens // rows,),
            in_specs=[
                pl.BlockSpec((rows, features), by_rows),
                pl.BlockSpec((1, features), lambda i, at: (0, 0)),
            ],
            out_specs=[
                pl.BlockSpec((rows, features), by_rows),
                pl.BlockSpec((rows, 1), by_rows),
                pl.BlockSpec((rows, features // 2), by_rows),
            ],
        ),
        out_shape=(
            jax.ShapeDtypeStruct(x.shape, jnp.bfloat16),
            jax.ShapeDtypeStruct((tokens, 1), jnp.float32),
            jax.ShapeDtypeStruct((tokens, features // 2), jnp.bfloat16),
        ),
        compiler_params=pltpu.CompilerParams(vmem_limit_bytes=12 * MIB),
        cost_estimate=cost(1, 1),
    )(places, x, gain)


def early_kernel(shards_ref, normed_ref, pair_ref, *refs, count):
    key_pieces = [pair_ref.at[0], *refs[: count - 1]]
    value_pieces = [pair_ref.at[1], *refs[count - 1 : 2 * count - 2]]
    key_ref, value_ref, key_w_ref, value_w_ref, key_sems, value_sems = refs[2 * count - 2 :]
    key_f, copies = add_rows(shards_ref, normed_ref, key_pieces, key_w_ref, key_sems, 0, None)
    value_f, more = add_rows(
        shards_ref, normed_ref, value_pieces, value_w_ref, value_sems, count, None
    )
    key_ref[...] = key_f
    value_ref[...] = value_f
    for copy in copies + more:
        copy.wait()


def early_rows(shards, normed, pair, key_pieces, value_pieces):
    tokens, features = normed.shape
    depth, width = key_pieces[0].shape
    count = len(key_pieces) + 1
    rows = jax.ShapeDtypeStruct((tokens, width), jnp.float32)
    whole = jax.ShapeDtypeStruct((features, width), jnp.bfloat16)
    return pl.pallas_call(
        lambda *refs: early_kernel(*refs, count=count),
        in_specs=[IN_SMEM] + in_vmem(2 * count),
        out_specs=in_vmem(2) + [ANYWHERE] * 2,
        out_shape=(rows, rows, whole, whole),
        scratch_shapes=[pltpu.SemaphoreType.DMA((count,))] * 2,
        compiler_params=pltpu.CompilerParams(vmem_limit_bytes=16 * MIB),
        cost_estimate=cost(1, 1),
    )(shards, normed, pair, *key_pieces, *value_pieces)


def attention_kernel(
    shards_ref, normed_ref, first_pair_ref, second_pair_ref, *refs, count, first, features
):
    key_pieces = [first_pair_ref.at[0], second_pair_ref.at[0], *refs[:count]]
    value_pieces = [first_pair_ref.at[1], second_pair_ref.at[1], *refs[count : 2 * count]]
    key_part_ref, value_part_ref, _, _, query_ref, grad_ref, seg_ref = refs[
        2 * count : 2 * count + 7
    ]
    key_w_ref, value_w_ref, grads_ref, inner_ref, key_sems, value_sems = refs[
        2 * count + 7 :
    ]
    key_f, copies = add_rows(
        shards_ref, normed_ref, key_pieces, key_w_ref, key_sems, first, key_part_ref[...]
    )
    value_f, more = add_rows(
        shards_ref, normed_ref, value_pieces, value_w_ref, value_sems, first + count + 2, value_part_ref[...]
    )
    tokens = query_ref.shape[0]
    width = key_f.shape[1]
    group_size = query_ref.shape[1] // width
    key_pos = lax.broadcasted_iota(jnp.int32, (tokens, tokens), 0)
    query_pos = lax.broadcasted_iota(jnp.int32, (tokens, tokens), 1)
    by_query = jnp.broadcast_to(seg_ref[...].astype(jnp.float32), (tokens, tokens))
    allowed = (key_pos <= query_pos) & (by_query.T == by_query)
    allowed = jnp.concatenate([jnp.where(allowed, 1.0, 0.0)] * group_size, 1) > 0.5
    total = jnp.zeros(inner_ref.shape, jnp.float32)
    for j in range(width // HD):
        at = slice(j * HD, (j + 1) * HD)
        key_j, value_j = key_f[:, at], value_f[:, at]
        query_j = stacked(query_ref, j, group_size)
        grad_j = stacked(grad_ref, j, group_size)
        scores = dot(key_j.astype(jnp.bfloat16), query_j, NT) * (HD ** (-0.5))
        scores = jnp.where(allowed, scores, jnp.float32(-1e30))
        weight = jnp.exp(scores - jnp.max(scores, 0, keepdims=True))
        probability = weight / jnp.sum(weight, 0, keepdims=True)
        value_grad = dot(probability.astype(jnp.bfloat16), grad_j, NN).astype(jnp.bfloat16)
        dprob = dot(value_j.astype(jnp.bfloat16), grad_j, NT)
        delta = jnp.sum(probability * dprob, 0, keepdims=True)
        dscore_b = (probability * (dprob - delta)).astype(jnp.bfloat16)
        key_grad = (dot(dscore_b, query_j, NN) * (HD ** (-0.5))).astype(jnp.bfloat16)
        grads_ref[:, at] = key_grad
        grads_ref[:, width + j * HD : width + (j + 1) * HD] = value_grad
        total = total + jnp.sum(
            key_grad.astype(jnp.float32) * key_j + value_grad.astype(jnp.float32) * value_j,
            1,
            keepdims=True,
        )
    inner_ref[...] = total / features
    for copy in copies + more:
        copy.wait()


def attention_grads(shards, first, normed, pairs, key_pieces, value_pieces, early, query, grad_out, segments):
    tokens, features = normed.shape
    depth, width = key_pieces[0].shape
    count = len(key_pieces)
    whole = jax.ShapeDtypeStruct((features, width), jnp.bfloat16)
    grads = jax.ShapeDtypeStruct((tokens, 2 * width), jnp.bfloat16)
    at = 2 * count + 6
    return pl.pallas_call(
        lambda *refs: attention_kernel(*refs, count=count, first=first, features=features),
        in_specs=[IN_SMEM] + in_vmem(2 * count + 5) + [ANYWHERE] * 2 + in_vmem(3),
        out_specs=[ANYWHERE] * 2 + in_vmem(2),
        out_shape=(whole, whole, grads, jax.ShapeDtypeStruct((tokens, 1), jnp.float32)),
        input_output_aliases={at: 0, at + 1: 1},
        scratch_shapes=[pltpu.SemaphoreType.DMA((count + 2,))] * 2,
        compiler_params=pltpu.CompilerParams(vmem_limit_bytes=20 * MIB),
        cost_estimate=cost(
            4 * tokens * depth * width * count + 8 * tokens * query.size,
            8 * depth * width * count + 4 * query.size,
            tokens * query.size // HD,
        ),
    )(shards, normed, *pairs, *key_pieces, *value_pieces, *early, query, grad_out, segments)


def pair_kernel(first_ref, second_ref, *rest):
    rest[-1][0] = first_ref[...]
    rest[-1][1] = second_ref[...]


def paired(first, second, *after):
    return pl.pallas_call(
        pair_kernel,
        in_specs=in_vmem(2) + [ANYWHERE] * len(after),
        out_specs=pl.BlockSpec(memory_space=pltpu.VMEM),
        out_shape=jax.ShapeDtypeStruct((2, *first.shape), first.dtype),
        compiler_params=pltpu.CompilerParams(vmem_limit_bytes=4 * MIB),
        cost_estimate=cost(1, 1),
    )(first, second, *after)


def branch_kernel(
    at_ref, grads_ref, key_w_ref, value_w_ref, x_ref, gain_ref, rms_ref, inner_ref, out_ref, *, half
):
    columns = key_w_ref.shape[1]
    key_grad, value_grad = grads_ref[:, :columns], grads_ref[:, columns:]
    rms = rms_ref[...]
    shift = rms * inner_ref[...]
    for i in range(out_ref.shape[1] // TILE):
        at = pl.ds(pl.multiple_of((at_ref[half] + i) * TILE, TILE), TILE)
        d_normed = dot(key_grad, key_w_ref[at, :], NT) + dot(value_grad, value_w_ref[at, :], NT)
        gated = gain_ref[:, at].astype(jnp.float32) * d_normed
        branch = rms * (gated - x_ref[:, at].astype(jnp.float32) * shift)
        out_ref[:, i * TILE : (i + 1) * TILE] = branch.astype(out_ref.dtype)


def partial_branch(places, half, kind, grads, key_w, value_w, x, gain, inv_rms, inner):
    tokens = grads.shape[0]
    columns = key_w.shape[1]
    width = TILE * HALF_TILES
    return pl.pallas_call(
        lambda *refs: branch_kernel(*refs, half=half),
        in_specs=[IN_SMEM] + in_vmem(7),
        out_specs=pl.BlockSpec(memory_space=pltpu.VMEM),
        out_shape=jax.ShapeDtypeStruct((tokens, width), kind),
        compiler_params=pltpu.CompilerParams(vmem_limit_bytes=20 * MIB),
        cost_estimate=cost(
            4 * tokens * width * columns, 4 * width * columns + 2 * width * tokens
        ),
    )(places, grads, key_w, value_w, x, gain, inv_rms, inner)


def weight_part_kernel(
    at_ref, normed_ref, normed_sib_ref, grads_ref, grads_sib_ref, after_ref,
    own_ref, right_ref, left_ref, far_right_ref, far_left_ref,
):
    grads = jnp.concatenate([grads_ref[...], grads_sib_ref[...]], 0)
    half = far_right_ref.shape[0]

    def part(step):
        k = lax.rem(at_ref[CHIP] + step, 4)
        own = pl.ds(pl.multiple_of((2 * k + at_ref[CORE]) * TILE, TILE), TILE)
        sib = pl.ds(pl.multiple_of(k * TILE, TILE), TILE)
        rows = jnp.concatenate([normed_ref[:, own], normed_sib_ref[:, sib]], 0)
        return dot(rows, grads, TN).astype(own_ref.dtype)

    far = part(2)
    far_right_ref[...] = far[:half]
    far_left_ref[...] = far[half:]
    own_ref[...] = part(0)
    right_ref[...] = part(1)
    left_ref[...] = part(3)


def weight_parts(places, normed, normed_sib, grads, grads_sib, after):
    part = jax.ShapeDtypeStruct((TILE, grads.shape[1]), jnp.bfloat16)
    half = jax.ShapeDtypeStruct((TILE // 2, grads.shape[1]), jnp.bfloat16)
    return pl.pallas_call(
        weight_part_kernel,
        in_specs=[IN_SMEM] + in_vmem(4) + [ANYWHERE],
        out_specs=in_vmem(5),
        out_shape=[part] * 3 + [half] * 2,
        compiler_params=pltpu.CompilerParams(vmem_limit_bytes=20 * MIB),
        cost_estimate=cost(4 * normed.size * grads.shape[1], 4 * normed.size),
    )(places, normed, normed_sib, grads, grads_sib, after)


def join_kernel(right_ref, left_ref, far_right_ref, far_left_ref, to_right_ref, to_left_ref, token_ref):
    half = far_right_ref.shape[0]
    join = lambda a, b: (a.astype(jnp.float32) + b.astype(jnp.float32)).astype(jnp.bfloat16)
    to_right_ref[:half] = join(right_ref[:half], far_right_ref[...])
    to_right_ref[half:] = right_ref[half:]
    to_left_ref[:half] = left_ref[:half]
    to_left_ref[half:] = join(left_ref[half:], far_left_ref[...])
    token_ref[...] = jnp.zeros_like(token_ref)


def join_parts(right, left, far_right, far_left):
    part = jax.ShapeDtypeStruct(right.shape, right.dtype)
    return pl.pallas_call(
        join_kernel,
        in_specs=in_vmem(4),
        out_specs=in_vmem(3),
        out_shape=[part, part, jax.ShapeDtypeStruct((8, 128), jnp.float32)],
        compiler_params=pltpu.CompilerParams(vmem_limit_bytes=12 * MIB),
        cost_estimate=cost(right.size, 8 * right.size),
    )(right, left, far_right, far_left)


def add_kernel(mine_ref, arrived_ref, token_ref, out_ref, held, sems):
    copies = []
    rows = held.shape[0] // sems.shape[0]
    for i in range(sems.shape[0]):
        at = pl.ds(i * rows, rows)
        held[at, :] = (mine_ref[at, :] + arrived_ref[at, :].astype(jnp.float32)).astype(held.dtype)
        copies.append(pltpu.make_async_copy(held.at[at, :], out_ref.at[at, :], sems.at[i]))
        copies[-1].start()
    for copy in copies:
        copy.wait()


def add_halves(mine, arrived, token):
    return pl.pallas_call(
        add_kernel,
        in_specs=in_vmem(2) + [ANYWHERE],
        out_specs=ANYWHERE,
        out_shape=jax.ShapeDtypeStruct(mine.shape, jnp.bfloat16),
        scratch_shapes=[
            pltpu.VMEM(mine.shape, jnp.bfloat16),
            pltpu.SemaphoreType.DMA((4,)),
        ],
        compiler_params=pltpu.CompilerParams(vmem_limit_bytes=8 * MIB),
        cost_estimate=cost(1e15, 1e12),
    )(mine, arrived, token)


def copy_kernel(at_ref, in_ref, out_ref):
    out_ref[...] = in_ref[...]


def take_rows(places, array, rows):
    width = array.shape[1]
    return pl.pallas_call(
        copy_kernel,
        grid_spec=pltpu.PrefetchScalarGridSpec(
            num_scalar_prefetch=1,
            grid=(1,),
            in_specs=[pl.BlockSpec((rows, width), lambda i, at: (at[STAGE], 0))],
            out_specs=pl.BlockSpec((rows, width), lambda i, at: (0, 0)),
        ),
        out_shape=jax.ShapeDtypeStruct((rows, width), array.dtype),
        compiler_params=pltpu.CompilerParams(vmem_limit_bytes=MIB),
        cost_estimate=cost(1, 1),
    )(places, array)


def suffix_kernel(parts_ref, top_ref, out_ref, held, sems):
    copies = []
    width = held.shape[2] // sems.shape[0]
    for i in range(sems.shape[0]):
        at = pl.ds(i * width, width)
        running = top_ref[:, at].astype(jnp.float32)
        for layer in reversed(range(parts_ref.shape[0])):
            running = running + parts_ref[layer, :, at].astype(jnp.float32)
            held[layer, :, at] = running.astype(jnp.bfloat16)
        copies.append(
            pltpu.make_async_copy(held.at[:, :, at], out_ref.at[:, :, at], sems.at[i])
        )
        copies[-1].start()
    for copy in copies:
        copy.wait()


def suffix_sum(parts, top):
    return pl.pallas_call(
        suffix_kernel,
        in_specs=in_vmem(2),
        out_specs=ANYWHERE,
        out_shape=jax.ShapeDtypeStruct(parts.shape, jnp.bfloat16),
        scratch_shapes=[
            pltpu.VMEM(parts.shape, jnp.bfloat16),
            pltpu.SemaphoreType.DMA((4,)),
        ],
        compiler_params=pltpu.CompilerParams(vmem_limit_bytes=8 * MIB),
        cost_estimate=cost(parts.size, 4 * parts.size),
    )(parts, top)


def move_kernel(in_ref, out_ref, held, in_sems, out_sems):
    count = in_sems.shape[0]
    rows = held.shape[0] // count
    arriving, leaving = [], []
    for i in range(count):
        at = pl.ds(i * rows, rows)
        arriving.append(pltpu.make_async_copy(in_ref.at[at, :], held.at[at, :], in_sems.at[i]))
        leaving.append(pltpu.make_async_copy(held.at[at, :], out_ref.at[at, :], out_sems.at[i]))
    for copy in arriving:
        copy.start()
    for i in range(count):
        arriving[i].wait()
        leaving[i].start()
    for copy in leaving:
        copy.wait()


def moved(array):
    return pl.pallas_call(
        move_kernel,
        in_specs=[ANYWHERE],
        out_specs=ANYWHERE,
        out_shape=jax.ShapeDtypeStruct(array.shape, array.dtype),
        scratch_shapes=[
            pltpu.VMEM(array.shape, array.dtype),
            pltpu.SemaphoreType.DMA((4,)),
            pltpu.SemaphoreType.DMA((4,)),
        ],
        compiler_params=pltpu.CompilerParams(vmem_limit_bytes=4 * MIB),
        cost_estimate=cost(1, 1),
    )(array)


def scale_kernel(factor_ref, *refs):
    *part_refs, out_ref = refs
    p = pl.program_id(0)
    for i in range(out_ref.shape[1] // BLOCK):
        for c in range(out_ref.shape[2] // HD):
            at = (slice(i * BLOCK, (i + 1) * BLOCK), slice(c * HD, (c + 1) * HD))
            total = part_refs[0][at].astype(jnp.float32)
            for ref in part_refs[1:]:
                total = total + ref[at].astype(jnp.float32)
            out_ref[(0, *at)] = (total * factor_ref[p, i, c]).astype(jnp.bfloat16)


def scaled_grad(parts, factor):
    rows = parts[0].shape[0]
    columns = parts[0].shape[1] // 2
    return pl.pallas_call(
        scale_kernel,
        grid=(2,),
        in_specs=[IN_SMEM] + [pl.BlockSpec((rows, columns), lambda p: (0, p))] * len(parts),
        out_specs=pl.BlockSpec((1, rows, columns), lambda p: (p, 0, 0)),
        out_shape=jax.ShapeDtypeStruct((2, rows, columns), jnp.bfloat16),
        compiler_params=pltpu.CompilerParams(vmem_limit_bytes=12 * MIB),
        cost_estimate=cost(1e15, 1e12),
    )(factor, *parts)


def ring_pairs(count):
    right = [(i, (i + 2) % count) for i in range(count)]
    left = [(i, (i - 2) % count) for i in range(count)]
    other = [(i, i ^ 1) for i in range(count)]
    return right, left, other


def on_device(
    layer_input, norm_gain, kv_weight, queries, out_grad, top_grad, segment_ids, scale_exp
):
    inputs = layer_input[0]
    token_count, feature_count = inputs.shape
    pipe_count = lax.axis_size("pipe")
    right, left, other = ring_pairs(lax.axis_size("dp"))
    send = lambda piece, pairs: lax.ppermute(piece, "dp", pairs)
    key_own, value_own = kv_weight[0, 0], kv_weight[0, 1]
    own_pair = send(kv_weight[0], other)
    key_l = send(key_own, right)
    value_r = send(value_own, left)
    key_r = send(key_own, left)
    value_l = send(value_own, right)
    places = all_places()
    normed, inv_rms, normed_other = norm(places, inputs, norm_gain)
    first_pair = send(paired(key_l, value_r, own_pair), other)
    key_2 = send(key_l, right)
    value_2 = send(value_r, left)
    early = early_rows(
        places,
        normed,
        own_pair,
        [key_own, key_l, key_r],
        [value_own, value_r, value_l],
    )
    normed_sib = send(normed_other, other)
    key_w, value_w, grads, inner = attention_grads(
        places,
        8,
        normed,
        [first_pair, send(paired(key_r, value_l, early[0]), other)],
        [key_2, send(key_2, other)],
        [value_2, send(value_2, other)],
        early,
        queries[0],
        out_grad[0],
        segment_ids[None, :],
    )

    def share(half, kind):
        return partial_branch(
            places, half, kind, grads, key_w, value_w, inputs, norm_gain, inv_rms, inner
        )

    arrived = lax.ppermute(share(THEIRS, jnp.bfloat16), "tensor", [(0, 1), (1, 0)])
    mine = share(MINE, jnp.float32)
    own, to_right, to_left, far_right, far_left = weight_parts(
        places, normed, normed_sib, grads, send(grads, other), mine
    )
    to_right, to_left, token = join_parts(
        to_right, to_left, send(far_right, right), send(far_left, left)
    )
    received = [send(to_right, right), send(to_left, left)]
    branch = add_halves(mine, arrived, token)
    parts = lax.all_to_all(branch, "pipe", 0, 0, tiled=True)
    rows = token_count // pipe_count
    sums = suffix_sum(
        parts.reshape(pipe_count, rows, branch.shape[1]), take_rows(places, top_grad, rows)
    )
    input_grad = lax.all_to_all(
        sums.reshape(token_count, branch.shape[1]), "pipe", 0, 0, tiled=True
    )
    weight_grad = scaled_grad([own, *received], jnp.exp2(-scale_exp[0].astype(jnp.float32)))
    return (moved(input_grad)[None], weight_grad[None])


def solution(mesh):
    placed = (
        P("pipe", "dp", None),
        P("pipe", None),
        P("pipe", None, "dp", "tensor"),
        P("pipe", "dp", "tensor"),
        P("pipe", "dp", "tensor"),
        P("dp", "tensor"),
        P("dp"),
        P("pipe", None, "dp", "tensor"),
    )
    return jax.shard_map(
        on_device,
        mesh=mesh,
        in_specs=placed,
        out_specs=(P("pipe", "dp", "tensor"), P("pipe", None, "dp", "tensor")),
        check_vma=False,
    )
```

```python
import jax
import jax.numpy as jnp
from jax import lax
from jax.experimental import pallas as pl
from jax.experimental.pallas import tpu as pltpu
from jax.sharding import PartitionSpec as P

HD = 128
BLOCK = 128
EPS = 1e-05
MIB = 1024 * 1024
TILE = 1024
HALF_TILES = 4
THEIRS, MINE, STAGE, CORE, CHIP = 16, 17, 18, 19, 20

NT = (((1,), (1,)), ((), ()))
NN = (((1,), (0,)), ((), ()))
TN = (((0,), (0,)), ((), ()))


def dot(a, b, dims):
    return lax.dot_general(a, b, dims, preferred_element_type=jnp.float32)


def cost(flops, nbytes, transcendentals=0):
    return pl.CostEstimate(
        flops=int(flops), bytes_accessed=int(nbytes), transcendentals=int(transcendentals)
    )


def stacked(ref, group, count):
    base = group * count
    return jnp.concatenate([ref[:, (base + h) * HD : (base + h + 1) * HD] for h in range(count)], 0)


def add_rows(shards_ref, normed_ref, pieces, whole_ref, sems, first, total):
    depth = pieces[0].shape[0]
    copies = []
    for i, piece in enumerate(pieces):
        rows = pl.ds(pl.multiple_of(shards_ref[first + i] * depth, depth), depth)
        copy = pltpu.make_async_copy(piece, whole_ref.at[rows, :], sems.at[i])
        copy.start()
        copies.append(copy)
    for i, piece in enumerate(pieces):
        columns = pl.ds(pl.multiple_of(shards_ref[first + i] * depth, depth), depth)
        part = dot(normed_ref[:, columns], piece[...], NN)
        total = part if total is None else total + part
    return total, copies


def in_vmem(count):
    return [pl.BlockSpec(memory_space=pltpu.VMEM)] * count


IN_SMEM = pl.BlockSpec(memory_space=pltpu.SMEM)
ANYWHERE = pl.BlockSpec(memory_space=pl.ANY)


def places_kernel(out_ref):
    me = lax.axis_index("dp")
    tensor_pos = lax.axis_index("tensor")
    before, after, across = lax.rem(me + 6, 8), lax.rem(me + 2, 8), lax.rem(me + 4, 8)
    sibling = lambda shard: shard + 1 - 2 * lax.rem(shard, 2)
    order = (sibling(me), me, before, after)
    order += (sibling(me), me, after, before)
    order += (sibling(before), sibling(after), across, sibling(across))
    order += (sibling(after), sibling(before), across, sibling(across))
    for i, shard in enumerate(order):
        out_ref[i] = shard
    out_ref[CORE] = lax.rem(me, 2)
    out_ref[CHIP] = me // 2
    out_ref[THEIRS] = (1 - tensor_pos) * HALF_TILES
    out_ref[MINE] = tensor_pos * HALF_TILES
    out_ref[STAGE] = lax.axis_index("pipe")


def all_places():
    return pl.pallas_call(
        places_kernel,
        out_specs=IN_SMEM,
        out_shape=jax.ShapeDtypeStruct((32,), jnp.int32),
        compiler_params=pltpu.CompilerParams(vmem_limit_bytes=MIB),
        cost_estimate=cost(1, 1),
    )()


def normed_kernel(at_ref, x_ref, gain_ref, normed_ref, rms_ref, other_ref):
    x = x_ref[...].astype(jnp.float32)
    rms = lax.rsqrt(jnp.mean(x * x, -1, keepdims=True) + EPS)
    rms_ref[...] = rms
    normed_ref[...] = ((x * rms) * gain_ref[...].astype(jnp.float32)).astype(jnp.bfloat16)
    for k in range(other_ref.shape[1] // TILE):
        shard = 2 * k + 1 - at_ref[CORE]
        columns = pl.ds(pl.multiple_of(shard * TILE, TILE), TILE)
        other_ref[:, k * TILE : (k + 1) * TILE] = normed_ref[:, columns]


def norm(places, x, gain):
    tokens, features = x.shape
    rows = min(tokens, 32)
    by_rows = lambda i, at: (i, 0)
    return pl.pallas_call(
        normed_kernel,
        grid_spec=pltpu.PrefetchScalarGridSpec(
            num_scalar_prefetch=1,
            grid=(tokens // rows,),
            in_specs=[
                pl.BlockSpec((rows, features), by_rows),
                pl.BlockSpec((1, features), lambda i, at: (0, 0)),
            ],
            out_specs=[
                pl.BlockSpec((rows, features), by_rows),
                pl.BlockSpec((rows, 1), by_rows),
                pl.BlockSpec((rows, features // 2), by_rows),
            ],
        ),
        out_shape=(
            jax.ShapeDtypeStruct(x.shape, jnp.bfloat16),
            jax.ShapeDtypeStruct((tokens, 1), jnp.float32),
            jax.ShapeDtypeStruct((tokens, features // 2), jnp.bfloat16),
        ),
        compiler_params=pltpu.CompilerParams(vmem_limit_bytes=12 * MIB),
        cost_estimate=cost(1, 1),
    )(places, x, gain)


def early_kernel(shards_ref, normed_ref, pair_ref, *refs, count):
    key_pieces = [pair_ref.at[0], *refs[: count - 1]]
    value_pieces = [pair_ref.at[1], *refs[count - 1 : 2 * count - 2]]
    key_ref, value_ref, key_w_ref, value_w_ref, key_sems, value_sems = refs[2 * count - 2 :]
    key_f, copies = add_rows(shards_ref, normed_ref, key_pieces, key_w_ref, key_sems, 0, None)
    value_f, more = add_rows(
        shards_ref, normed_ref, value_pieces, value_w_ref, value_sems, count, None
    )
    key_ref[...] = key_f
    value_ref[...] = value_f
    for copy in copies + more:
        copy.wait()


def early_rows(shards, normed, pair, key_pieces, value_pieces):
    tokens, features = normed.shape
    depth, width = key_pieces[0].shape
    count = len(key_pieces) + 1
    rows = jax.ShapeDtypeStruct((tokens, width), jnp.float32)
    whole = jax.ShapeDtypeStruct((features, width), jnp.bfloat16)
    return pl.pallas_call(
        lambda *refs: early_kernel(*refs, count=count),
        in_specs=[IN_SMEM] + in_vmem(2 * count),
        out_specs=in_vmem(2) + [ANYWHERE] * 2,
        out_shape=(rows, rows, whole, whole),
        scratch_shapes=[pltpu.SemaphoreType.DMA((count,))] * 2,
        compiler_params=pltpu.CompilerParams(vmem_limit_bytes=16 * MIB),
        cost_estimate=cost(1, 1),
    )(shards, normed, pair, *key_pieces, *value_pieces)


def attention_kernel(
    shards_ref, normed_ref, first_pair_ref, second_pair_ref, *refs, count, first, features
):
    key_pieces = [first_pair_ref.at[0], second_pair_ref.at[0], *refs[:count]]
    value_pieces = [first_pair_ref.at[1], second_pair_ref.at[1], *refs[count : 2 * count]]
    key_part_ref, value_part_ref, _, _, query_ref, grad_ref, seg_ref = refs[
        2 * count : 2 * count + 7
    ]
    key_w_ref, value_w_ref, grads_ref, inner_ref, key_sems, value_sems = refs[
        2 * count + 7 :
    ]
    key_f, copies = add_rows(
        shards_ref, normed_ref, key_pieces, key_w_ref, key_sems, first, key_part_ref[...]
    )
    value_f, more = add_rows(
        shards_ref, normed_ref, value_pieces, value_w_ref, value_sems, first + count + 2, value_part_ref[...]
    )
    tokens = query_ref.shape[0]
    width = key_f.shape[1]
    group_size = query_ref.shape[1] // width
    key_pos = lax.broadcasted_iota(jnp.int32, (tokens, tokens), 0)
    query_pos = lax.broadcasted_iota(jnp.int32, (tokens, tokens), 1)
    by_query = jnp.broadcast_to(seg_ref[...].astype(jnp.float32), (tokens, tokens))
    allowed = (key_pos <= query_pos) & (by_query.T == by_query)
    allowed = jnp.concatenate([jnp.where(allowed, 1.0, 0.0)] * group_size, 1) > 0.5
    total = jnp.zeros(inner_ref.shape, jnp.float32)
    for j in range(width // HD):
        at = slice(j * HD, (j + 1) * HD)
        key_j, value_j = key_f[:, at], value_f[:, at]
        query_j = stacked(query_ref, j, group_size)
        grad_j = stacked(grad_ref, j, group_size)
        scores = dot(key_j.astype(jnp.bfloat16), query_j, NT) * (HD ** (-0.5))
        scores = jnp.where(allowed, scores, jnp.float32(-1e30))
        weight = jnp.exp(scores - jnp.max(scores, 0, keepdims=True))
        probability = weight / jnp.sum(weight, 0, keepdims=True)
        value_grad = dot(probability.astype(jnp.bfloat16), grad_j, NN).astype(jnp.bfloat16)
        dprob = dot(value_j.astype(jnp.bfloat16), grad_j, NT)
        delta = jnp.sum(probability * dprob, 0, keepdims=True)
        dscore_b = (probability * (dprob - delta)).astype(jnp.bfloat16)
        key_grad = (dot(dscore_b, query_j, NN) * (HD ** (-0.5))).astype(jnp.bfloat16)
        grads_ref[:, at] = key_grad
        grads_ref[:, width + j * HD : width + (j + 1) * HD] = value_grad
        total = total + jnp.sum(
            key_grad.astype(jnp.float32) * key_j + value_grad.astype(jnp.float32) * value_j,
            1,
            keepdims=True,
        )
    inner_ref[...] = total / features
    for copy in copies + more:
        copy.wait()


def attention_grads(shards, first, normed, pairs, key_pieces, value_pieces, early, query, grad_out, segments):
    tokens, features = normed.shape
    depth, width = key_pieces[0].shape
    count = len(key_pieces)
    whole = jax.ShapeDtypeStruct((features, width), jnp.bfloat16)
    grads = jax.ShapeDtypeStruct((tokens, 2 * width), jnp.bfloat16)
    at = 2 * count + 6
    return pl.pallas_call(
        lambda *refs: attention_kernel(*refs, count=count, first=first, features=features),
        in_specs=[IN_SMEM] + in_vmem(2 * count + 5) + [ANYWHERE] * 2 + in_vmem(3),
        out_specs=[ANYWHERE] * 2 + in_vmem(2),
        out_shape=(whole, whole, grads, jax.ShapeDtypeStruct((tokens, 1), jnp.float32)),
        input_output_aliases={at: 0, at + 1: 1},
        scratch_shapes=[pltpu.SemaphoreType.DMA((count + 2,))] * 2,
        compiler_params=pltpu.CompilerParams(vmem_limit_bytes=20 * MIB),
        cost_estimate=cost(
            4 * tokens * depth * width * count + 8 * tokens * query.size,
            8 * depth * width * count + 4 * query.size,
            tokens * query.size // HD,
        ),
    )(shards, normed, *pairs, *key_pieces, *value_pieces, *early, query, grad_out, segments)


def pair_kernel(first_ref, second_ref, *rest):
    rest[-1][0] = first_ref[...]
    rest[-1][1] = second_ref[...]


def paired(first, second, *after):
    return pl.pallas_call(
        pair_kernel,
        in_specs=in_vmem(2) + [ANYWHERE] * len(after),
        out_specs=pl.BlockSpec(memory_space=pltpu.VMEM),
        out_shape=jax.ShapeDtypeStruct((2, *first.shape), first.dtype),
        compiler_params=pltpu.CompilerParams(vmem_limit_bytes=4 * MIB),
        cost_estimate=cost(1, 1),
    )(first, second, *after)


def branch_kernel(
    at_ref, grads_ref, key_w_ref, value_w_ref, x_ref, gain_ref, rms_ref, inner_ref, out_ref, *, half
):
    columns = key_w_ref.shape[1]
    key_grad, value_grad = grads_ref[:, :columns], grads_ref[:, columns:]
    rms = rms_ref[...]
    shift = rms * inner_ref[...]
    for i in range(out_ref.shape[1] // TILE):
        at = pl.ds(pl.multiple_of((at_ref[half] + i) * TILE, TILE), TILE)
        d_normed = dot(key_grad, key_w_ref[at, :], NT) + dot(value_grad, value_w_ref[at, :], NT)
        gated = gain_ref[:, at].astype(jnp.float32) * d_normed
        branch = rms * (gated - x_ref[:, at].astype(jnp.float32) * shift)
        out_ref[:, i * TILE : (i + 1) * TILE] = branch.astype(out_ref.dtype)


def partial_branch(places, half, kind, grads, key_w, value_w, x, gain, inv_rms, inner):
    tokens = grads.shape[0]
    columns = key_w.shape[1]
    width = TILE * HALF_TILES
    return pl.pallas_call(
        lambda *refs: branch_kernel(*refs, half=half),
        in_specs=[IN_SMEM] + in_vmem(7),
        out_specs=pl.BlockSpec(memory_space=pltpu.VMEM),
        out_shape=jax.ShapeDtypeStruct((tokens, width), kind),
        compiler_params=pltpu.CompilerParams(vmem_limit_bytes=20 * MIB),
        cost_estimate=cost(
            4 * tokens * width * columns, 4 * width * columns + 2 * width * tokens
        ),
    )(places, grads, key_w, value_w, x, gain, inv_rms, inner)


def weight_part_kernel(
    at_ref, normed_ref, normed_sib_ref, grads_ref, grads_sib_ref, after_ref,
    own_ref, right_ref, left_ref, far_right_ref, far_left_ref,
):
    grads = jnp.concatenate([grads_ref[...], grads_sib_ref[...]], 0)
    half = far_right_ref.shape[0]

    def part(step):
        k = lax.rem(at_ref[CHIP] + step, 4)
        own = pl.ds(pl.multiple_of((2 * k + at_ref[CORE]) * TILE, TILE), TILE)
        sib = pl.ds(pl.multiple_of(k * TILE, TILE), TILE)
        rows = jnp.concatenate([normed_ref[:, own], normed_sib_ref[:, sib]], 0)
        return dot(rows, grads, TN).astype(own_ref.dtype)

    far = part(2)
    far_right_ref[...] = far[:half]
    far_left_ref[...] = far[half:]
    own_ref[...] = part(0)
    right_ref[...] = part(1)
    left_ref[...] = part(3)


def weight_parts(places, normed, normed_sib, grads, grads_sib, after):
    part = jax.ShapeDtypeStruct((TILE, grads.shape[1]), jnp.bfloat16)
    half = jax.ShapeDtypeStruct((TILE // 2, grads.shape[1]), jnp.bfloat16)
    return pl.pallas_call(
        weight_part_kernel,
        in_specs=[IN_SMEM] + in_vmem(4) + [ANYWHERE],
        out_specs=in_vmem(5),
        out_shape=[part] * 3 + [half] * 2,
        compiler_params=pltpu.CompilerParams(vmem_limit_bytes=20 * MIB),
        cost_estimate=cost(4 * normed.size * grads.shape[1], 4 * normed.size),
    )(places, normed, normed_sib, grads, grads_sib, after)


def join_kernel(right_ref, left_ref, far_right_ref, far_left_ref, to_right_ref, to_left_ref, token_ref):
    half = far_right_ref.shape[0]
    join = lambda a, b: (a.astype(jnp.float32) + b.astype(jnp.float32)).astype(jnp.bfloat16)
    to_right_ref[:half] = join(right_ref[:half], far_right_ref[...])
    to_right_ref[half:] = right_ref[half:]
    to_left_ref[:half] = left_ref[:half]
    to_left_ref[half:] = join(left_ref[half:], far_left_ref[...])
    token_ref[...] = jnp.zeros_like(token_ref)


def join_parts(right, left, far_right, far_left):
    part = jax.ShapeDtypeStruct(right.shape, right.dtype)
    return pl.pallas_call(
        join_kernel,
        in_specs=in_vmem(4),
        out_specs=in_vmem(3),
        out_shape=[part, part, jax.ShapeDtypeStruct((8, 128), jnp.float32)],
        compiler_params=pltpu.CompilerParams(vmem_limit_bytes=12 * MIB),
        cost_estimate=cost(right.size, 8 * right.size),
    )(right, left, far_right, far_left)


def add_kernel(mine_ref, arrived_ref, token_ref, out_ref, held, sems):
    copies = []
    rows = held.shape[0] // sems.shape[0]
    for i in range(sems.shape[0]):
        at = pl.ds(i * rows, rows)
        held[at, :] = (mine_ref[at, :] + arrived_ref[at, :].astype(jnp.float32)).astype(held.dtype)
        copies.append(pltpu.make_async_copy(held.at[at, :], out_ref.at[at, :], sems.at[i]))
        copies[-1].start()
    for copy in copies:
        copy.wait()


def add_halves(mine, arrived, token):
    return pl.pallas_call(
        add_kernel,
        in_specs=in_vmem(2) + [ANYWHERE],
        out_specs=ANYWHERE,
        out_shape=jax.ShapeDtypeStruct(mine.shape, jnp.bfloat16),
        scratch_shapes=[
            pltpu.VMEM(mine.shape, jnp.bfloat16),
            pltpu.SemaphoreType.DMA((4,)),
        ],
        compiler_params=pltpu.CompilerParams(vmem_limit_bytes=8 * MIB),
        cost_estimate=cost(1e15, 1e12),
    )(mine, arrived, token)


def top_kernel(at_ref, in_ref, out_ref):
    half = out_ref.shape[0]
    both = in_ref[...].astype(jnp.float32)
    out_ref[...] = jnp.where(lax.rem(at_ref[STAGE], 2) == 0, both[:half], both[half:])


def take_rows(places, array, rows):
    width = array.shape[1]
    return pl.pallas_call(
        top_kernel,
        grid_spec=pltpu.PrefetchScalarGridSpec(
            num_scalar_prefetch=1,
            grid=(1,),
            in_specs=[pl.BlockSpec((2 * rows, width), lambda i, at: (at[STAGE] // 2, 0))],
            out_specs=pl.BlockSpec((rows, width), lambda i, at: (0, 0)),
        ),
        out_shape=jax.ShapeDtypeStruct((rows, width), jnp.float32),
        compiler_params=pltpu.CompilerParams(vmem_limit_bytes=2 * MIB),
        cost_estimate=cost(1, 1),
    )(places, array)


def suffix_kernel(parts_ref, top_ref, out_ref, held, sems):
    copies = []
    rows = top_ref.shape[0]
    width = held.shape[1] // sems.shape[0]
    for i in range(sems.shape[0]):
        at = pl.ds(i * width, width)
        running = top_ref[:, at]
        for first in reversed(range(0, held.shape[0], 2 * rows)):
            two = pl.ds(first, 2 * rows)
            layers = parts_ref[two, at].astype(jnp.float32)
            later = running + layers[rows:]
            running = later + layers[:rows]
            held[two, at] = jnp.concatenate([running, later], 0).astype(jnp.bfloat16)
        copies.append(pltpu.make_async_copy(held.at[:, at], out_ref.at[:, at], sems.at[i]))
        copies[-1].start()
    for copy in copies:
        copy.wait()


def suffix_sum(parts, top):
    return pl.pallas_call(
        suffix_kernel,
        in_specs=in_vmem(2),
        out_specs=ANYWHERE,
        out_shape=jax.ShapeDtypeStruct(parts.shape, jnp.bfloat16),
        scratch_shapes=[
            pltpu.VMEM(parts.shape, jnp.bfloat16),
            pltpu.SemaphoreType.DMA((4,)),
        ],
        compiler_params=pltpu.CompilerParams(vmem_limit_bytes=8 * MIB),
        cost_estimate=cost(parts.size, 4 * parts.size),
    )(parts, top)


def move_kernel(in_ref, out_ref, held, in_sems, out_sems):
    count = in_sems.shape[0]
    rows = held.shape[0] // count
    arriving, leaving = [], []
    for i in range(count):
        at = pl.ds(i * rows, rows)
        arriving.append(pltpu.make_async_copy(in_ref.at[at, :], held.at[at, :], in_sems.at[i]))
        leaving.append(pltpu.make_async_copy(held.at[at, :], out_ref.at[at, :], out_sems.at[i]))
    for copy in arriving:
        copy.start()
    for i in range(count):
        arriving[i].wait()
        leaving[i].start()
    for copy in leaving:
        copy.wait()


def moved(array):
    return pl.pallas_call(
        move_kernel,
        in_specs=[ANYWHERE],
        out_specs=ANYWHERE,
        out_shape=jax.ShapeDtypeStruct(array.shape, array.dtype),
        scratch_shapes=[
            pltpu.VMEM(array.shape, array.dtype),
            pltpu.SemaphoreType.DMA((4,)),
            pltpu.SemaphoreType.DMA((4,)),
        ],
        compiler_params=pltpu.CompilerParams(vmem_limit_bytes=4 * MIB),
        cost_estimate=cost(1, 1),
    )(array)


def scale_kernel(factor_ref, *refs):
    *part_refs, out_ref = refs
    p = pl.program_id(0)
    for i in range(out_ref.shape[1] // BLOCK):
        for c in range(out_ref.shape[2] // HD):
            at = (slice(i * BLOCK, (i + 1) * BLOCK), slice(c * HD, (c + 1) * HD))
            total = part_refs[0][at].astype(jnp.float32)
            for ref in part_refs[1:]:
                total = total + ref[at].astype(jnp.float32)
            out_ref[(0, *at)] = (total * factor_ref[p, i, c]).astype(jnp.bfloat16)


def scaled_grad(parts, factor):
    rows = parts[0].shape[0]
    columns = parts[0].shape[1] // 2
    return pl.pallas_call(
        scale_kernel,
        grid=(2,),
        in_specs=[IN_SMEM] + [pl.BlockSpec((rows, columns), lambda p: (0, p))] * len(parts),
        out_specs=pl.BlockSpec((1, rows, columns), lambda p: (p, 0, 0)),
        out_shape=jax.ShapeDtypeStruct((2, rows, columns), jnp.bfloat16),
        compiler_params=pltpu.CompilerParams(vmem_limit_bytes=12 * MIB),
        cost_estimate=cost(1e15, 1e12),
    )(factor, *parts)


def ring_pairs(count):
    right = [(i, (i + 2) % count) for i in range(count)]
    left = [(i, (i - 2) % count) for i in range(count)]
    other = [(i, i ^ 1) for i in range(count)]
    return right, left, other


def on_device(
    layer_input, norm_gain, kv_weight, queries, out_grad, top_grad, segment_ids, scale_exp
):
    inputs = layer_input[0]
    token_count, feature_count = inputs.shape
    pipe_count = lax.axis_size("pipe")
    right, left, other = ring_pairs(lax.axis_size("dp"))
    send = lambda piece, pairs: lax.ppermute(piece, "dp", pairs)
    key_own, value_own = kv_weight[0, 0], kv_weight[0, 1]
    own_pair = send(kv_weight[0], other)
    key_l = send(key_own, right)
    value_r = send(value_own, left)
    key_r = send(key_own, left)
    value_l = send(value_own, right)
    places = all_places()
    normed, inv_rms, normed_other = norm(places, inputs, norm_gain)
    first_pair = send(paired(key_l, value_r, own_pair), other)
    key_2 = send(key_l, right)
    value_2 = send(value_r, left)
    early = early_rows(
        places,
        normed,
        own_pair,
        [key_own, key_l, key_r],
        [value_own, value_r, value_l],
    )
    normed_sib = send(normed_other, other)
    key_w, value_w, grads, inner = attention_grads(
        places,
        8,
        normed,
        [first_pair, send(paired(key_r, value_l, early[0]), other)],
        [key_2, send(key_2, other)],
        [value_2, send(value_2, other)],
        early,
        queries[0],
        out_grad[0],
        segment_ids[None, :],
    )

    def share(half, kind):
        return partial_branch(
            places, half, kind, grads, key_w, value_w, inputs, norm_gain, inv_rms, inner
        )

    arrived = lax.ppermute(share(THEIRS, jnp.bfloat16), "tensor", [(0, 1), (1, 0)])
    mine = share(MINE, jnp.float32)
    own, to_right, to_left, far_right, far_left = weight_parts(
        places, normed, normed_sib, grads, send(grads, other), mine
    )
    to_right, to_left, token = join_parts(
        to_right, to_left, send(far_right, right), send(far_left, left)
    )
    received = [send(to_right, right), send(to_left, left)]
    branch = add_halves(mine, arrived, token)
    parts = lax.all_to_all(branch, "pipe", 0, 0, tiled=True)
    rows = token_count // pipe_count
    sums = suffix_sum(parts, take_rows(places, top_grad, rows))
    input_grad = lax.all_to_all(sums, "pipe", 0, 0, tiled=True)
    weight_grad = scaled_grad([own, *received], jnp.exp2(-scale_exp[0].astype(jnp.float32)))
    return (moved(input_grad)[None], weight_grad[None])


def solution(mesh):
    placed = (
        P("pipe", "dp", None),
        P("pipe", None),
        P("pipe", None, "dp", "tensor"),
        P("pipe", "dp", "tensor"),
        P("pipe", "dp", "tensor"),
        P("dp", "tensor"),
        P("dp"),
        P("pipe", None, "dp", "tensor"),
    )
    return jax.shard_map(
        on_device,
        mesh=mesh,
        in_specs=placed,
        out_specs=(P("pipe", "dp", "tensor"), P("pipe", None, "dp", "tensor")),
        check_vma=False,
    )
```

```python
import jax
import jax.numpy as jnp
from jax import lax
from jax.experimental import pallas as pl
from jax.experimental.pallas import tpu as pltpu
from jax.sharding import PartitionSpec as P

HD = 128
BLOCK = 128
EPS = 1e-05
MIB = 1024 * 1024
TILE = 1024
HALF_TILES = 4
THEIRS, MINE, STAGE, CORE, CHIP = 16, 17, 18, 19, 20

NT = (((1,), (1,)), ((), ()))
NN = (((1,), (0,)), ((), ()))
TN = (((0,), (0,)), ((), ()))


def dot(a, b, dims):
    return lax.dot_general(a, b, dims, preferred_element_type=jnp.float32)


def cost(flops, nbytes, transcendentals=0):
    return pl.CostEstimate(
        flops=int(flops), bytes_accessed=int(nbytes), transcendentals=int(transcendentals)
    )


def stacked(ref, group, count):
    base = group * count
    return jnp.concatenate([ref[:, (base + h) * HD : (base + h + 1) * HD] for h in range(count)], 0)


def add_rows(shards_ref, normed_ref, pieces, whole_ref, sems, first, total):
    depth = pieces[0].shape[0]
    copies = []
    for i, piece in enumerate(pieces):
        rows = pl.ds(pl.multiple_of(shards_ref[first + i] * depth, depth), depth)
        copy = pltpu.make_async_copy(piece, whole_ref.at[rows, :], sems.at[i])
        copy.start()
        copies.append(copy)
    for i, piece in enumerate(pieces):
        columns = pl.ds(pl.multiple_of(shards_ref[first + i] * depth, depth), depth)
        part = dot(normed_ref[:, columns], piece[...], NN)
        total = part if total is None else total + part
    return total, copies


def in_vmem(count):
    return [pl.BlockSpec(memory_space=pltpu.VMEM)] * count


IN_SMEM = pl.BlockSpec(memory_space=pltpu.SMEM)
ANYWHERE = pl.BlockSpec(memory_space=pl.ANY)


def places_kernel(out_ref):
    me = lax.axis_index("dp")
    tensor_pos = lax.axis_index("tensor")
    before, after, across = lax.rem(me + 6, 8), lax.rem(me + 2, 8), lax.rem(me + 4, 8)
    sibling = lambda shard: shard + 1 - 2 * lax.rem(shard, 2)
    order = (sibling(me), me, before, after)
    order += (sibling(me), me, after, before)
    order += (sibling(before), sibling(after), across, sibling(across))
    order += (sibling(after), sibling(before), across, sibling(across))
    for i, shard in enumerate(order):
        out_ref[i] = shard
    out_ref[CORE] = lax.rem(me, 2)
    out_ref[CHIP] = me // 2
    out_ref[THEIRS] = (1 - tensor_pos) * HALF_TILES
    out_ref[MINE] = tensor_pos * HALF_TILES
    out_ref[STAGE] = lax.axis_index("pipe")


def all_places():
    return pl.pallas_call(
        places_kernel,
        out_specs=IN_SMEM,
        out_shape=jax.ShapeDtypeStruct((32,), jnp.int32),
        compiler_params=pltpu.CompilerParams(vmem_limit_bytes=MIB),
        cost_estimate=cost(1, 1),
    )()


def normed_kernel(at_ref, x_ref, gain_ref, normed_ref, rms_ref, other_ref):
    x = x_ref[...].astype(jnp.float32)
    rms = lax.rsqrt(jnp.mean(x * x, -1, keepdims=True) + EPS)
    rms_ref[...] = rms
    normed_ref[...] = ((x * rms) * gain_ref[...].astype(jnp.float32)).astype(jnp.bfloat16)
    for k in range(other_ref.shape[1] // TILE):
        shard = 2 * k + 1 - at_ref[CORE]
        columns = pl.ds(pl.multiple_of(shard * TILE, TILE), TILE)
        other_ref[:, k * TILE : (k + 1) * TILE] = normed_ref[:, columns]


def norm(places, x, gain):
    tokens, features = x.shape
    rows = min(tokens, 32)
    by_rows = lambda i, at: (i, 0)
    return pl.pallas_call(
        normed_kernel,
        grid_spec=pltpu.PrefetchScalarGridSpec(
            num_scalar_prefetch=1,
            grid=(tokens // rows,),
            in_specs=[
                pl.BlockSpec((rows, features), by_rows),
                pl.BlockSpec((1, features), lambda i, at: (0, 0)),
            ],
            out_specs=[
                pl.BlockSpec((rows, features), by_rows),
                pl.BlockSpec((rows, 1), by_rows),
                pl.BlockSpec((rows, features // 2), by_rows),
            ],
        ),
        out_shape=(
            jax.ShapeDtypeStruct(x.shape, jnp.bfloat16),
            jax.ShapeDtypeStruct((tokens, 1), jnp.float32),
            jax.ShapeDtypeStruct((tokens, features // 2), jnp.bfloat16),
        ),
        compiler_params=pltpu.CompilerParams(vmem_limit_bytes=12 * MIB),
        cost_estimate=cost(1, 1),
    )(places, x, gain)


def early_kernel(shards_ref, normed_ref, pair_ref, *refs, count):
    key_pieces = [pair_ref.at[0], *refs[: count - 1]]
    value_pieces = [pair_ref.at[1], *refs[count - 1 : 2 * count - 2]]
    key_ref, value_ref, key_w_ref, value_w_ref, key_sems, value_sems = refs[2 * count - 2 :]
    key_f, copies = add_rows(shards_ref, normed_ref, key_pieces, key_w_ref, key_sems, 0, None)
    value_f, more = add_rows(
        shards_ref, normed_ref, value_pieces, value_w_ref, value_sems, count, None
    )
    key_ref[...] = key_f
    value_ref[...] = value_f
    for copy in copies + more:
        copy.wait()


def early_rows(shards, normed, pair, key_pieces, value_pieces):
    tokens, features = normed.shape
    depth, width = key_pieces[0].shape
    count = len(key_pieces) + 1
    rows = jax.ShapeDtypeStruct((tokens, width), jnp.float32)
    whole = jax.ShapeDtypeStruct((features, width), jnp.bfloat16)
    return pl.pallas_call(
        lambda *refs: early_kernel(*refs, count=count),
        in_specs=[IN_SMEM] + in_vmem(2 * count),
        out_specs=in_vmem(2) + [ANYWHERE] * 2,
        out_shape=(rows, rows, whole, whole),
        scratch_shapes=[pltpu.SemaphoreType.DMA((count,))] * 2,
        compiler_params=pltpu.CompilerParams(vmem_limit_bytes=16 * MIB),
        cost_estimate=cost(1, 1),
    )(shards, normed, pair, *key_pieces, *value_pieces)


def attention_kernel(
    shards_ref, normed_ref, first_pair_ref, second_pair_ref, *refs, count, first, features
):
    key_pieces = [first_pair_ref.at[0], second_pair_ref.at[0], *refs[:count]]
    value_pieces = [first_pair_ref.at[1], second_pair_ref.at[1], *refs[count : 2 * count]]
    key_part_ref, value_part_ref, _, _, query_ref, grad_ref, seg_ref = refs[
        2 * count : 2 * count + 7
    ]
    key_w_ref, value_w_ref, grads_ref, inner_ref, key_sems, value_sems = refs[
        2 * count + 7 :
    ]
    key_f, copies = add_rows(
        shards_ref, normed_ref, key_pieces, key_w_ref, key_sems, first, key_part_ref[...]
    )
    value_f, more = add_rows(
        shards_ref, normed_ref, value_pieces, value_w_ref, value_sems, first + count + 2, value_part_ref[...]
    )
    tokens = query_ref.shape[0]
    width = key_f.shape[1]
    group_size = query_ref.shape[1] // width
    key_pos = lax.broadcasted_iota(jnp.int32, (tokens, tokens), 0)
    query_pos = lax.broadcasted_iota(jnp.int32, (tokens, tokens), 1)
    by_query = jnp.broadcast_to(seg_ref[...].astype(jnp.float32), (tokens, tokens))
    allowed = (key_pos <= query_pos) & (by_query.T == by_query)
    allowed = jnp.concatenate([jnp.where(allowed, 1.0, 0.0)] * group_size, 1) > 0.5
    total = jnp.zeros(inner_ref.shape, jnp.float32)
    for j in range(width // HD):
        at = slice(j * HD, (j + 1) * HD)
        key_j, value_j = key_f[:, at], value_f[:, at]
        query_j = stacked(query_ref, j, group_size)
        grad_j = stacked(grad_ref, j, group_size)
        scores = dot(key_j.astype(jnp.bfloat16), query_j, NT) * (HD ** (-0.5))
        scores = jnp.where(allowed, scores, jnp.float32(-1e30))
        weight = jnp.exp(scores - jnp.max(scores, 0, keepdims=True))
        probability = weight / jnp.sum(weight, 0, keepdims=True)
        value_grad = dot(probability.astype(jnp.bfloat16), grad_j, NN).astype(jnp.bfloat16)
        dprob = dot(value_j.astype(jnp.bfloat16), grad_j, NT)
        delta = jnp.sum(probability * dprob, 0, keepdims=True)
        dscore_b = (probability * (dprob - delta)).astype(jnp.bfloat16)
        key_grad = (dot(dscore_b, query_j, NN) * (HD ** (-0.5))).astype(jnp.bfloat16)
        grads_ref[:, at] = key_grad
        grads_ref[:, width + j * HD : width + (j + 1) * HD] = value_grad
        total = total + jnp.sum(
            key_grad.astype(jnp.float32) * key_j + value_grad.astype(jnp.float32) * value_j,
            1,
            keepdims=True,
        )
    inner_ref[...] = total / features
    for copy in copies + more:
        copy.wait()


def attention_grads(shards, first, normed, pairs, key_pieces, value_pieces, early, query, grad_out, segments):
    tokens, features = normed.shape
    depth, width = key_pieces[0].shape
    count = len(key_pieces)
    whole = jax.ShapeDtypeStruct((features, width), jnp.bfloat16)
    grads = jax.ShapeDtypeStruct((tokens, 2 * width), jnp.bfloat16)
    at = 2 * count + 6
    return pl.pallas_call(
        lambda *refs: attention_kernel(*refs, count=count, first=first, features=features),
        in_specs=[IN_SMEM] + in_vmem(2 * count + 5) + [ANYWHERE] * 2 + in_vmem(3),
        out_specs=[ANYWHERE] * 2 + in_vmem(2),
        out_shape=(whole, whole, grads, jax.ShapeDtypeStruct((tokens, 1), jnp.float32)),
        input_output_aliases={at: 0, at + 1: 1},
        scratch_shapes=[pltpu.SemaphoreType.DMA((count + 2,))] * 2,
        compiler_params=pltpu.CompilerParams(vmem_limit_bytes=20 * MIB),
        cost_estimate=cost(
            4 * tokens * depth * width * count + 8 * tokens * query.size,
            8 * depth * width * count + 4 * query.size,
            tokens * query.size // HD,
        ),
    )(shards, normed, *pairs, *key_pieces, *value_pieces, *early, query, grad_out, segments)


def pair_kernel(first_ref, second_ref, *rest):
    rest[-1][0] = first_ref[...]
    rest[-1][1] = second_ref[...]


def paired(first, second, *after):
    return pl.pallas_call(
        pair_kernel,
        in_specs=in_vmem(2) + [ANYWHERE] * len(after),
        out_specs=pl.BlockSpec(memory_space=pltpu.VMEM),
        out_shape=jax.ShapeDtypeStruct((2, *first.shape), first.dtype),
        compiler_params=pltpu.CompilerParams(vmem_limit_bytes=4 * MIB),
        cost_estimate=cost(1, 1),
    )(first, second, *after)


def branch_kernel(
    at_ref, grads_ref, key_w_ref, value_w_ref, x_ref, gain_ref, rms_ref, inner_ref, out_ref, *, half
):
    columns = key_w_ref.shape[1]
    key_grad, value_grad = grads_ref[:, :columns], grads_ref[:, columns:]
    rms = rms_ref[...]
    shift = rms * inner_ref[...]
    for i in range(out_ref.shape[1] // TILE):
        at = pl.ds(pl.multiple_of((at_ref[half] + i) * TILE, TILE), TILE)
        d_normed = dot(key_grad, key_w_ref[at, :], NT) + dot(value_grad, value_w_ref[at, :], NT)
        gated = gain_ref[:, at].astype(jnp.float32) * d_normed
        branch = rms * (gated - x_ref[:, at].astype(jnp.float32) * shift)
        out_ref[:, i * TILE : (i + 1) * TILE] = branch.astype(out_ref.dtype)


def partial_branch(places, half, kind, grads, key_w, value_w, x, gain, inv_rms, inner):
    tokens = grads.shape[0]
    columns = key_w.shape[1]
    width = TILE * HALF_TILES
    return pl.pallas_call(
        lambda *refs: branch_kernel(*refs, half=half),
        in_specs=[IN_SMEM] + in_vmem(7),
        out_specs=pl.BlockSpec(memory_space=pltpu.VMEM),
        out_shape=jax.ShapeDtypeStruct((tokens, width), kind),
        compiler_params=pltpu.CompilerParams(vmem_limit_bytes=20 * MIB),
        cost_estimate=cost(
            4 * tokens * width * columns, 4 * width * columns + 2 * width * tokens
        ),
    )(places, grads, key_w, value_w, x, gain, inv_rms, inner)


def weight_part_kernel(
    at_ref, normed_ref, normed_sib_ref, grads_ref, grads_sib_ref, after_ref,
    own_ref, right_ref, left_ref, far_right_ref, far_left_ref,
):
    grads = jnp.concatenate([grads_ref[...], grads_sib_ref[...]], 0)
    half = far_right_ref.shape[0]

    def part(step):
        k = lax.rem(at_ref[CHIP] + step, 4)
        own = pl.ds(pl.multiple_of((2 * k + at_ref[CORE]) * TILE, TILE), TILE)
        sib = pl.ds(pl.multiple_of(k * TILE, TILE), TILE)
        rows = jnp.concatenate([normed_ref[:, own], normed_sib_ref[:, sib]], 0)
        return dot(rows, grads, TN).astype(own_ref.dtype)

    far = part(2)
    far_right_ref[...] = far[:half]
    far_left_ref[...] = far[half:]
    own_ref[...] = part(0)
    right_ref[...] = part(1)
    left_ref[...] = part(3)


def weight_parts(places, normed, normed_sib, grads, grads_sib, after):
    part = jax.ShapeDtypeStruct((TILE, grads.shape[1]), jnp.bfloat16)
    half = jax.ShapeDtypeStruct((TILE // 2, grads.shape[1]), jnp.bfloat16)
    return pl.pallas_call(
        weight_part_kernel,
        in_specs=[IN_SMEM] + in_vmem(4) + [ANYWHERE],
        out_specs=in_vmem(5),
        out_shape=[part] * 3 + [half] * 2,
        compiler_params=pltpu.CompilerParams(vmem_limit_bytes=20 * MIB),
        cost_estimate=cost(4 * normed.size * grads.shape[1], 4 * normed.size),
    )(places, normed, normed_sib, grads, grads_sib, after)


def join_kernel(right_ref, left_ref, far_right_ref, far_left_ref, to_right_ref, to_left_ref, token_ref):
    half = far_right_ref.shape[0]
    join = lambda a, b: (a.astype(jnp.float32) + b.astype(jnp.float32)).astype(jnp.bfloat16)
    to_right_ref[:half] = join(right_ref[:half], far_right_ref[...])
    to_right_ref[half:] = right_ref[half:]
    to_left_ref[:half] = left_ref[:half]
    to_left_ref[half:] = join(left_ref[half:], far_left_ref[...])
    token_ref[...] = jnp.zeros_like(token_ref)


def join_parts(right, left, far_right, far_left):
    part = jax.ShapeDtypeStruct(right.shape, right.dtype)
    return pl.pallas_call(
        join_kernel,
        in_specs=in_vmem(4),
        out_specs=in_vmem(3),
        out_shape=[part, part, jax.ShapeDtypeStruct((8, 128), jnp.float32)],
        compiler_params=pltpu.CompilerParams(vmem_limit_bytes=12 * MIB),
        cost_estimate=cost(right.size, 8 * right.size),
    )(right, left, far_right, far_left)


def add_kernel(mine_ref, arrived_ref, token_ref, out_ref, held, sems):
    copies = []
    rows = held.shape[0] // sems.shape[0]
    for i in range(sems.shape[0]):
        at = pl.ds(i * rows, rows)
        held[at, :] = (mine_ref[at, :] + arrived_ref[at, :].astype(jnp.float32)).astype(held.dtype)
        copies.append(pltpu.make_async_copy(held.at[at, :], out_ref.at[at, :], sems.at[i]))
        copies[-1].start()
    for copy in copies:
        copy.wait()


def add_halves(mine, arrived, token):
    return pl.pallas_call(
        add_kernel,
        in_specs=in_vmem(2) + [ANYWHERE],
        out_specs=ANYWHERE,
        out_shape=jax.ShapeDtypeStruct(mine.shape, jnp.bfloat16),
        scratch_shapes=[
            pltpu.VMEM(mine.shape, jnp.bfloat16),
            pltpu.SemaphoreType.DMA((4,)),
        ],
        compiler_params=pltpu.CompilerParams(vmem_limit_bytes=8 * MIB),
        cost_estimate=cost(1e15, 1e12),
    )(mine, arrived, token)


def top_kernel(at_ref, in_ref, out_ref):
    half = out_ref.shape[0]
    both = in_ref[...].astype(jnp.float32)
    out_ref[...] = jnp.where(lax.rem(at_ref[STAGE], 2) == 0, both[:half], both[half:])


def take_rows(places, array, rows):
    width = array.shape[1]
    return pl.pallas_call(
        top_kernel,
        grid_spec=pltpu.PrefetchScalarGridSpec(
            num_scalar_prefetch=1,
            grid=(1,),
            in_specs=[pl.BlockSpec((2 * rows, width), lambda i, at: (at[STAGE] // 2, 0))],
            out_specs=pl.BlockSpec((rows, width), lambda i, at: (0, 0)),
        ),
        out_shape=jax.ShapeDtypeStruct((rows, width), jnp.float32),
        compiler_params=pltpu.CompilerParams(vmem_limit_bytes=2 * MIB),
        cost_estimate=cost(1, 1),
    )(places, array)


def suffix_kernel(parts_ref, top_ref, out_ref, held, sems):
    copies = []
    rows = top_ref.shape[0]
    width = held.shape[1] // sems.shape[0]
    for i in range(sems.shape[0]):
        at = pl.ds(i * width, width)
        running = top_ref[:, at]
        for first in reversed(range(0, held.shape[0], 2 * rows)):
            two = pl.ds(first, 2 * rows)
            layers = parts_ref[two, at].astype(jnp.float32)
            later = running + layers[rows:]
            running = later + layers[:rows]
            held[two, at] = jnp.concatenate([running, later], 0).astype(jnp.bfloat16)
        copies.append(pltpu.make_async_copy(held.at[:, at], out_ref.at[:, at], sems.at[i]))
        copies[-1].start()
    for copy in copies:
        copy.wait()


def suffix_sum(parts, top):
    return pl.pallas_call(
        suffix_kernel,
        in_specs=in_vmem(2),
        out_specs=ANYWHERE,
        out_shape=jax.ShapeDtypeStruct(parts.shape, jnp.bfloat16),
        scratch_shapes=[
            pltpu.VMEM(parts.shape, jnp.bfloat16),
            pltpu.SemaphoreType.DMA((4,)),
        ],
        compiler_params=pltpu.CompilerParams(vmem_limit_bytes=8 * MIB),
        cost_estimate=cost(parts.size, 4 * parts.size),
    )(parts, top)


def move_kernel(in_ref, out_ref, held, in_sems, out_sems):
    count = in_sems.shape[0]
    rows = held.shape[0] // count
    arriving, leaving = [], []
    for i in range(count):
        at = pl.ds(i * rows, rows)
        arriving.append(pltpu.make_async_copy(in_ref.at[at, :], held.at[at, :], in_sems.at[i]))
        leaving.append(pltpu.make_async_copy(held.at[at, :], out_ref.at[at, :], out_sems.at[i]))
    for copy in arriving:
        copy.start()
    for i in range(count):
        arriving[i].wait()
        leaving[i].start()
    for copy in leaving:
        copy.wait()


def moved(array):
    return pl.pallas_call(
        move_kernel,
        in_specs=[ANYWHERE],
        out_specs=ANYWHERE,
        out_shape=jax.ShapeDtypeStruct(array.shape, array.dtype),
        scratch_shapes=[
            pltpu.VMEM(array.shape, array.dtype),
            pltpu.SemaphoreType.DMA((8,)),
            pltpu.SemaphoreType.DMA((8,)),
        ],
        compiler_params=pltpu.CompilerParams(vmem_limit_bytes=4 * MIB),
        cost_estimate=cost(1, 1),
    )(array)


def scale_kernel(factor_ref, *refs):
    *part_refs, out_ref = refs
    p = pl.program_id(0)
    for i in range(out_ref.shape[1] // BLOCK):
        for c in range(out_ref.shape[2] // HD):
            at = (slice(i * BLOCK, (i + 1) * BLOCK), slice(c * HD, (c + 1) * HD))
            total = part_refs[0][at].astype(jnp.float32)
            for ref in part_refs[1:]:
                total = total + ref[at].astype(jnp.float32)
            out_ref[(0, *at)] = (total * factor_ref[p, i, c]).astype(jnp.bfloat16)


def scaled_grad(parts, factor):
    rows = parts[0].shape[0]
    columns = parts[0].shape[1] // 2
    return pl.pallas_call(
        scale_kernel,
        grid=(2,),
        in_specs=[IN_SMEM] + [pl.BlockSpec((rows, columns), lambda p: (0, p))] * len(parts),
        out_specs=pl.BlockSpec((1, rows, columns), lambda p: (p, 0, 0)),
        out_shape=jax.ShapeDtypeStruct((2, rows, columns), jnp.bfloat16),
        compiler_params=pltpu.CompilerParams(vmem_limit_bytes=12 * MIB),
        cost_estimate=cost(1e15, 1e12),
    )(factor, *parts)


def ring_pairs(count):
    right = [(i, (i + 2) % count) for i in range(count)]
    left = [(i, (i - 2) % count) for i in range(count)]
    other = [(i, i ^ 1) for i in range(count)]
    return right, left, other


def on_device(
    layer_input, norm_gain, kv_weight, queries, out_grad, top_grad, segment_ids, scale_exp
):
    inputs = layer_input[0]
    token_count, feature_count = inputs.shape
    pipe_count = lax.axis_size("pipe")
    right, left, other = ring_pairs(lax.axis_size("dp"))
    send = lambda piece, pairs: lax.ppermute(piece, "dp", pairs)
    key_own, value_own = kv_weight[0, 0], kv_weight[0, 1]
    own_pair = send(kv_weight[0], other)
    key_l = send(key_own, right)
    value_r = send(value_own, left)
    key_r = send(key_own, left)
    value_l = send(value_own, right)
    places = all_places()
    normed, inv_rms, normed_other = norm(places, inputs, norm_gain)
    first_pair = send(paired(key_l, value_r, own_pair), other)
    key_2 = send(key_l, right)
    value_2 = send(value_r, left)
    early = early_rows(
        places,
        normed,
        own_pair,
        [key_own, key_l, key_r],
        [value_own, value_r, value_l],
    )
    normed_sib = send(normed_other, other)
    key_w, value_w, grads, inner = attention_grads(
        places,
        8,
        normed,
        [first_pair, send(paired(key_r, value_l, early[0]), other)],
        [key_2, send(key_2, other)],
        [value_2, send(value_2, other)],
        early,
        queries[0],
        out_grad[0],
        segment_ids[None, :],
    )

    def share(half, kind):
        return partial_branch(
            places, half, kind, grads, key_w, value_w, inputs, norm_gain, inv_rms, inner
        )

    arrived = lax.ppermute(share(THEIRS, jnp.bfloat16), "tensor", [(0, 1), (1, 0)])
    mine = share(MINE, jnp.float32)
    own, to_right, to_left, far_right, far_left = weight_parts(
        places, normed, normed_sib, grads, send(grads, other), mine
    )
    to_right, to_left, token = join_parts(
        to_right, to_left, send(far_right, right), send(far_left, left)
    )
    received = [send(to_right, right), send(to_left, left)]
    branch = add_halves(mine, arrived, token)
    parts = lax.all_to_all(branch, "pipe", 0, 0, tiled=True)
    rows = token_count // pipe_count
    sums = suffix_sum(parts, take_rows(places, top_grad, rows))
    input_grad = lax.all_to_all(sums, "pipe", 0, 0, tiled=True)
    weight_grad = scaled_grad([own, *received], jnp.exp2(-scale_exp[0].astype(jnp.float32)))
    return (moved(input_grad)[None], weight_grad[None])


def solution(mesh):
    placed = (
        P("pipe", "dp", None),
        P("pipe", None),
        P("pipe", None, "dp", "tensor"),
        P("pipe", "dp", "tensor"),
        P("pipe", "dp", "tensor"),
        P("dp", "tensor"),
        P("dp"),
        P("pipe", None, "dp", "tensor"),
    )
    return jax.shard_map(
        on_device,
        mesh=mesh,
        in_specs=placed,
        out_specs=(P("pipe", "dp", "tensor"), P("pipe", None, "dp", "tensor")),
        check_vma=False,
    )
```
